32 devices in a mesh: rep: 8 (over y, x, core), tp: 4 (over z).
Axes of the slice: x: 2, y: 2, z: 4, core: 2. Of those that a mesh axis runs over, the one named last changes fastest.
Arguments:
- queries: bfloat16 [104, 48, 4096], P('rep', None, 'tp'), may hold values from -33 to 33
- tree_cache: bfloat16 [104, 2, 48, 4096], P('rep', None, None, 'tp'), may hold values from -11 to 11
- tree_mask: int32 [104, 48, 48], P('rep'), may hold values from 0 to 1, as said below
- dest_group: int32 [104, 1], P('rep'), may hold values from 0 to 7; in each aligned block of 13 rows (0 to 12, 13 to 25, ...) at most 2 rows name the same one
- accepted_path: int32 [104, 8], P('rep'), may hold values from 0 to 47
- prompt_cache: bfloat16 [8, 2, 152, 4096], P('rep', None, None, 'tp'), may hold values from -11 to 11
- first_len: int32 [8], P('rep'), may hold values from 2 to 152
- spill_cache: bfloat16 [8, 2, 152, 4096], P('rep', None, None, 'tp'), may hold values from -6 to 6
- spill_len: int32 [8], P('rep'), may hold values from 76 to 152
- out_weight: bfloat16 [4096, 4096], P(None, 'tp'), may hold values from -0.09375 to 0.09375
Outputs:
- projected: bfloat16 [104, 48, 4096], P('rep', None, 'tp')
- accepted_cache: bfloat16 [104, 2, 8, 4096], P('rep', None, None, 'tp')
The draws below stay inside these ranges and needn't reach their ends.
Inputs may be any that keep to these rules, and one draw needn't show every extreme that they name: `dest_group`: in each aligned block of 13 requests (those of one index of rep) no group is named more than 2 times. Row t of tree_mask[r] marks token t and its ancestors in a tree whose parents come before their children.
All inputs are finite; a program needn't handle non-finite values.
Results may differ from the reference program's by a relative error of at most 0.014.
Values may be sent and summed in bfloat16 or wider, within the bound.
No kernel may reach another device: no remote copies, remote signals or barrier semaphores. Data moves between devices by JAX's collectives and lax.ppermute only.
A program may use at most 128 MiB of HBM per device.

```python
import math
from functools import partial
import jax
import jax.numpy as jnp
import numpy as np
from jax import lax

HD = 128
HEADS = 32
DW = 4096
TREE = 48
ACC = 8
PCAP = 152
REQ_DEV = 13
CAP = 2
REQUESTS = 104
GROUPS = 8
C = 4096


def draw_queries(key, part):
    base_key = jax.random.fold_in(key, 11)
    values = jnp.clip(jax.random.normal(base_key, (REQUESTS, TREE, HEADS * HD), jnp.float32), -4.5, 4.5)
    return values.astype(jnp.bfloat16)


def draw_prompt_cache(key, part):
    base_key = jax.random.fold_in(key, 17)
    values = jnp.clip(jax.random.normal(base_key, (GROUPS, 2, PCAP, HEADS * HD), jnp.float32), -4.5, 4.5)
    return values.astype(jnp.bfloat16)


def draw_tree_cache(key, part):
    base_key = jax.random.fold_in(key, 19)
    values = jnp.clip(jax.random.normal(base_key, (REQUESTS, 2, TREE, HEADS * HD), jnp.float32), -6.0, 6.0)
    return values.astype(jnp.bfloat16)


def draw_tree_mask(key, part):
    limits = jnp.maximum(jnp.arange(TREE, dtype=jnp.int32), 1)
    parents = jax.random.randint(key, (REQUESTS, TREE), 0, limits[None, :])

    def build_rows(parent_row):

        def extend(mask_rows, token):
            new_row = mask_rows[parent_row[token]].at[token].set(1)
            return (mask_rows.at[token].set(new_row), None)
        mask_rows, unused = lax.scan(extend, jnp.zeros((TREE, TREE), jnp.int32), jnp.arange(TREE, dtype=jnp.int32))
        return mask_rows
    return jax.vmap(build_rows)(parents)


def draw_first_len(key, part):
    lengths = jax.random.randint(key, (GROUPS,), 2, PCAP + 1)
    chosen = jax.random.randint(jax.random.fold_in(key, 3), (), 0, GROUPS)
    return lengths.at[chosen].set(PCAP)


def draw_spill_len(key, part):
    lengths = jax.random.randint(key, (GROUPS,), PCAP // 2, PCAP + 1)
    chosen = jax.random.randint(jax.random.fold_in(key, 3), (), 0, GROUPS)
    return lengths.at[chosen].set(PCAP)


def place_ends(values, rng, smallest, high):
    extent = values.shape
    index_at = [jax.random.randint(jax.random.fold_in(rng, axis), (), 0, extent[axis]) for axis in range(len(extent))]
    values = values.at[tuple(index_at)].set(smallest)
    longest = extent.index(max(extent))
    index_at[longest] = (index_at[longest] + 1) % extent[longest]
    return values.at[tuple(index_at)].set(high)


def block_levels(own_key, shape, pieces, low, largest):
    def one(axis_at, blocks):
        heights = jax.random.uniform(jax.random.fold_in(jax.random.fold_in(own_key, 6), axis_at), (blocks,), jnp.float32, low / len(pieces), largest / len(pieces))
        return jnp.repeat(jnp.exp(heights), shape[axis_at] // blocks).reshape((-1,) + (1,) * (len(shape) - axis_at - 1))

    gain = one(*pieces[0])
    for cut in pieces[1:]:
        gain = gain * one(*cut)
    return gain


def assign_block(stream_key, own, number, rows, number_of, top, limit, lean):
    order = jax.random.permutation(stream_key, number_of)
    crowded, common = shares(number_of, rows * top, limit, lean, True), shares(number_of, rows * top, limit, lean, False)
    places = jnp.arange(number_of)

    def named(sizes, rotation):
        used = int((sizes > 0).sum())
        fixed = max(1, used // 4)
        moved = fixed + (places - fixed + rotation * (used - fixed)) % max(1, number_of - fixed)
        return jnp.zeros((number_of,), jnp.int32).at[order[jnp.where(places < fixed, places, moved)]].set(jnp.asarray(sizes, jnp.int32))

    sizes = jnp.where(number % 4 == 0, named(crowded, number // 4), named(common, number - number // 4 - 1))
    mixed = jax.random.permutation(jax.random.fold_in(own, 3), number_of)
    source_of, taker = mixed[0:number_of // 2 * 2:2], mixed[1:number_of // 2 * 2:2]
    room = jnp.minimum(sizes[source_of] - 1, limit - sizes[taker]) // 2
    room = jnp.where((source_of == order[0]) | (taker == order[0]) | (sizes[taker] == 0), 0, jnp.maximum(room, 0))
    moved = jax.random.randint(jax.random.fold_in(own, 4), (number_of // 2,), 0, 1 << 20) % (room + 1)
    sizes = sizes.at[source_of].add(-moved).at[taker].add(moved)
    items = jnp.searchsorted(jnp.cumsum(sizes), jnp.arange(rows * top), side="right").astype(jnp.int32)
    table = items.reshape(top, rows).T
    table = table[jax.random.permutation(jax.random.fold_in(own, 1), rows)]
    rotation = jax.random.randint(jax.random.fold_in(own, 2), (rows, 1), 0, top)
    return jnp.take_along_axis(table, (jnp.arange(top)[None, :] + rotation) % top, axis=1)


def shares(number_of, total, bound, lean, full):
    weights = [(1 << 20) // math.isqrt(standing ** lean) + 1 for standing in range(1, number_of + 1)]
    largest = bound if full else min(bound, max(-(-total // number_of), total * weights[0] // sum(weights)))
    least = 1 if total - largest >= number_of - 1 else 0
    given, spare = [largest] + [least] * (number_of - 1), total - largest - least * (number_of - 1)
    while spare > 0:
        free = [i for i in range(1, number_of) if given[i] < largest] or [i for i in range(1, number_of) if given[i] < bound]
        pool, budget = sum([weights[i] for i in free]), spare
        for i in free:
            extra = min(bound - given[i], max(1, budget * weights[i] // pool), spare)
            given[i] = given[i] + extra
            spare = spare - extra
    return np.array(given)


def normal_values(stream_key, dims, spread, reach, shards=(), held_as=jnp.bfloat16):
    gain = block_levels(stream_key, dims, shards, -0.22, 0.18) if shards else 1.0
    entries = jax.random.normal(stream_key, dims, jnp.float32) * spread * gain
    return jnp.minimum(jnp.maximum(entries, -reach), reach).astype(held_as)


def setup_inputs(seed: int = 0) -> dict:
    key_list = jax.random.split(jax.random.key(seed), 11)
    queries = draw_queries(jax.random.fold_in(key_list[10], 71), 0)
    tree_cache = draw_tree_cache(jax.random.fold_in(key_list[10], 71), 0)
    tree_mask = draw_tree_mask(jax.random.fold_in(key_list[10], 71), 0)
    dest_group_keys = jax.random.split(jax.random.fold_in(key_list[3], 1), REQUESTS // REQ_DEV)
    dest_group_turns = jax.random.permutation(jax.random.fold_in(key_list[3], 3), REQUESTS // REQ_DEV)
    dest_group = jax.vmap(lambda own, number: assign_block(jax.random.fold_in(key_list[3], 2), own, number, REQ_DEV, GROUPS, 1, CAP, 2))(dest_group_keys, dest_group_turns).reshape((REQUESTS, 1))
    accepted_path = place_ends(jax.random.randint(key_list[4], (REQUESTS, ACC), 0, TREE), jax.random.fold_in(key_list[4], 1), 0, TREE - 1).astype(jnp.int32)
    prompt_cache = draw_prompt_cache(jax.random.fold_in(key_list[10], 71), 0)
    first_len = draw_first_len(jax.random.fold_in(key_list[10], 71), 0)
    spill_cache = normal_values(key_list[7], (GROUPS, 2, PCAP, C), 1.0, 6.0, ((0, 8), (3, 4)))
    spill_len = draw_spill_len(jax.random.fold_in(key_list[10], 71), 0)
    out_weight = normal_values(key_list[9], (C, DW), C ** -0.5, 0.09375, ((1, 4),))
    return dict(queries=queries, tree_cache=tree_cache, tree_mask=tree_mask, dest_group=dest_group, accepted_path=accepted_path, prompt_cache=prompt_cache, first_len=first_len, spill_cache=spill_cache, spill_len=spill_len, out_weight=out_weight)


NEG_FILL = -1e+30

def attend_request(inputs, prompt_cache, first_len, spill_cache, spill_len):
    query_block, tree_block, mask_block, group_id = inputs
    partner_id = jnp.bitwise_xor(group_id, 1).astype(jnp.int32)
    prompt_block = prompt_cache[group_id]
    spill_block = spill_cache[partner_id]
    positions = jnp.arange(PCAP, dtype=jnp.int32)
    prompt_seen = positions < first_len[group_id]
    spill_seen = positions < spill_len[partner_id]
    key_rows = jnp.concatenate([prompt_block[0], spill_block[0], tree_block[0]], axis=0).astype(jnp.float32)
    value_rows = jnp.concatenate([prompt_block[1], spill_block[1], tree_block[1]], axis=0).astype(jnp.float32)
    visible = jnp.concatenate([jnp.broadcast_to(prompt_seen[None, :], (TREE, PCAP)), jnp.broadcast_to(spill_seen[None, :], (TREE, PCAP)), mask_block == 1], axis=1)
    query_heads = query_block.astype(jnp.float32).reshape(TREE, HEADS, HD)
    key_heads = key_rows.reshape(-1, HEADS, HD)
    value_heads = value_rows.reshape(-1, HEADS, HD)
    scores = jnp.einsum('thd,lhd->htl', query_heads, key_heads) * (1.0 / math.sqrt(HD))
    scores = jnp.where(visible[None], scores, NEG_FILL)
    peaks = lax.optimization_barrier(jnp.max(scores, axis=2, keepdims=True))
    raw_weights = jnp.where(visible[None], jnp.exp(scores - peaks), 0.0)
    totals = lax.optimization_barrier(jnp.sum(raw_weights, axis=2))
    rounded = lax.optimization_barrier(raw_weights.astype(jnp.bfloat16)).astype(jnp.float32)
    accum = jnp.einsum('htl,lhd->thd', rounded, value_heads)
    attn = accum / jnp.transpose(totals)[:, :, None]
    return attn.reshape(TREE, HEADS * HD).astype(jnp.bfloat16)

def reference(queries, tree_cache, tree_mask, dest_group, accepted_path, prompt_cache, first_len, spill_cache, spill_len, out_weight):
    worker = partial(attend_request, prompt_cache=prompt_cache, first_len=first_len, spill_cache=spill_cache, spill_len=spill_len)
    attn = lax.map(worker, (queries, tree_cache, tree_mask, dest_group[:, 0].astype(jnp.int32)))
    flat_attn = attn.reshape(REQUESTS * TREE, HEADS * HD)
    projected = jnp.dot(flat_attn, out_weight, preferred_element_type=jnp.float32).astype(jnp.bfloat16)
    projected = projected.reshape(REQUESTS, TREE, DW)
    accepted_cache = jnp.take_along_axis(tree_cache, accepted_path[:, None, :, None].astype(jnp.int32), axis=2)
    return (projected, accepted_cache)
```

```python
import math
from functools import partial

import jax
import jax.numpy as jnp
from jax import lax
from jax.experimental import pallas as pl
from jax.experimental.pallas import tpu as pltpu
from jax.sharding import PartitionSpec as P

HD = 128
NEG_FILL = -1e30
SCALE = 1.0 / math.sqrt(HD)
VMEM_BYTES = 48 * 1024 * 1024


def attend_kernel(idx_ref, q_ref, tree_ref, bias_ref, *rest, n_caches):
    cache_refs = rest[:n_caches]
    out_ref, held, sems = rest[n_caches:]
    copies = []
    at = 0
    for i, ref in enumerate(cache_refs):
        size = ref.shape[0]
        copies.append(pltpu.make_async_copy(ref, held.at[pl.ds(at, size)], sems.at[i]))
        at += size
    for copy in copies:
        copy.start()
    for copy in copies:
        copy.wait()
    requests, _, width = q_ref.shape
    padded = held.shape[3]
    n_keys = bias_ref.shape[2]
    position = lax.broadcasted_iota(jnp.int32, (1, n_keys), 1).astype(jnp.float32)
    repeats = -(-n_keys // HD)

    def length_row(block, part):
        tail = held[block, part, 0, pl.ds(padded - 16, 16), 0:HD].astype(jnp.float32)[15:16]
        return jnp.concatenate([tail] * repeats, axis=1)[:, :n_keys]

    def body(r, carry):
        first = idx_ref[0, r]
        second = idx_ref[1, r]
        limit = jnp.where(position < padded, length_row(first, 0), length_row(second, 1) + padded)
        limit = jnp.where(position < 2 * padded, limit, n_keys)
        bias = bias_ref[r] + jnp.where(position < limit, 0.0, NEG_FILL)
        for h in range(width // HD):
            cols = slice(h * HD, (h + 1) * HD)
            keys = jnp.concatenate(
                [held[first, 0, 0, :, cols], held[second, 1, 0, :, cols], tree_ref[r, 0, :, cols]], axis=0
            )
            values = jnp.concatenate(
                [held[first, 0, 1, :, cols], held[second, 1, 1, :, cols], tree_ref[r, 1, :, cols]], axis=0
            )
            scores = lax.dot_general(
                q_ref[r, :, cols], keys, (((1,), (1,)), ((), ())), preferred_element_type=jnp.float32
            )
            scores = scores * SCALE + bias
            raw = jnp.exp(scores - jnp.max(scores, axis=1, keepdims=True))
            total = jnp.sum(raw, axis=1, keepdims=True)
            accum = jnp.dot(raw.astype(jnp.bfloat16), values, preferred_element_type=jnp.float32)
            out_ref[r, :, cols] = (accum / total).astype(out_ref.dtype)
        return carry

    lax.fori_loop(0, requests, body, 0)


def attend(idx, queries, tree_cache, bias, caches, start, width):
    req, tree, _ = queries.shape
    block = start // width
    n_blocks = sum(c.shape[0] for c in caches)
    keys = bias.shape[2]
    return pl.pallas_call(
        partial(attend_kernel, n_caches=len(caches)),
        grid=(1,),
        in_specs=[
            pl.BlockSpec(memory_space=pltpu.SMEM),
            pl.BlockSpec((req, tree, width), lambda i: (0, 0, block)),
            pl.BlockSpec((req, 2, tree, width), lambda i: (0, 0, 0, block)),
            pl.BlockSpec(bias.shape, lambda i: (0, 0, 0)),
        ]
        + [pl.BlockSpec(memory_space=pl.ANY)] * len(caches),
        out_specs=pl.BlockSpec((req, tree, width), lambda i: (0, 0, 0)),
        out_shape=jax.ShapeDtypeStruct((req, tree, width), jnp.bfloat16),
        scratch_shapes=[
            pltpu.VMEM((n_blocks,) + caches[0].shape[1:], jnp.bfloat16),
            pltpu.SemaphoreType.DMA((len(caches),)),
        ],
        compiler_params=pltpu.CompilerParams(vmem_limit_bytes=VMEM_BYTES),
        cost_estimate=pl.CostEstimate(
            flops=4 * req * tree * keys * width * 16, bytes_accessed=8 * n_blocks * 320 * width, transcendentals=0
        ),
    )(idx, queries, tree_cache, bias, *caches)


def project_kernel(z_ref, own, p1, p2, p3, p4, p5, w_ref, *rest, has_acc):
    out_ref = rest[-1]
    z = z_ref[0]
    middle = jnp.logical_and(z > 0, z < 3)
    lower = z < 2
    src_a = jnp.where(lower, 2, 1)
    src_b = jnp.where(lower, 3, 0)
    total = jnp.dot(own[...], w_ref[z], preferred_element_type=jnp.float32)
    total += jnp.dot(p1[...], w_ref[jnp.bitwise_xor(z, 1)], preferred_element_type=jnp.float32)
    total += jnp.dot(jnp.where(middle, p2[...], p4[...]), w_ref[src_a], preferred_element_type=jnp.float32)
    total += jnp.dot(jnp.where(middle, p3[...], p5[...]), w_ref[src_b], preferred_element_type=jnp.float32)
    if has_acc:
        total += rest[0][...]
    out_ref[...] = total.astype(out_ref.dtype)


def project(z, pieces, weight, acc, start, width, last):
    rows = pieces[0].shape[0]
    _, _, cols = weight.shape
    tile = 256
    block = start // width
    whole = pl.BlockSpec((rows, width), lambda n: (0, 0))
    args = [z, *pieces, weight] + ([acc] if acc is not None else [])
    out_type = jnp.bfloat16 if last else jnp.float32
    in_place = {7 + 1: 0} if acc is not None and not last else {}
    return pl.pallas_call(
        partial(project_kernel, has_acc=acc is not None),
        grid=(cols // tile,),
        in_specs=[pl.BlockSpec(memory_space=pltpu.SMEM)]
        + [whole] * 6
        + [pl.BlockSpec((weight.shape[0], width, tile), lambda n: (0, block, n))]
        + ([pl.BlockSpec((rows, tile), lambda n: (0, n))] if acc is not None else []),
        out_specs=pl.BlockSpec((rows, tile), lambda n: (0, n)),
        out_shape=jax.ShapeDtypeStruct((rows, cols), out_type),
        input_output_aliases=in_place,
        compiler_params=pltpu.CompilerParams(vmem_limit_bytes=VMEM_BYTES),
        cost_estimate=pl.CostEstimate(
            flops=2 * rows * 4 * width * cols, bytes_accessed=8 * width * cols + 8 * rows * cols, transcendentals=0
        ),
    )(*args)


def cache_block(prompt_cache, spill_cache, lens, start, width, padded):
    both = jnp.stack([prompt_cache[..., start : start + width], spill_cache[..., start : start + width]], axis=1)
    both = jnp.pad(both, ((0, 0), (0, 0), (0, 0), (0, padded - both.shape[3]), (0, 0)))
    row = lax.broadcasted_iota(jnp.int32, both.shape, 3)
    return jnp.where(row == padded - 1, lens[None, :, None, None, None], both)


def gather_caches(block):
    def across(value, mask):
        return lax.ppermute(value, "rep", [(i, i ^ mask) for i in range(lax.axis_size("rep"))])

    same = [block] + [across(block, m) for m in (2, 4, 6)]
    other = [across(value, 1) for value in same]
    return [value for pair in zip(same, other) for value in pair]


def exchange(attn):
    def send(value, pairs):
        return lax.ppermute(value, "tp", pairs)

    p1 = send(attn, [(0, 1), (1, 0), (2, 3), (3, 2)])
    p2 = send(attn, [(1, 2), (2, 1)])
    p3 = send(p1, [(1, 2), (2, 1)])
    p4 = send(p2, [(1, 0), (2, 3)])
    p5 = send(p3, [(1, 0), (2, 3)])
    return [attn, p1, p2, p3, p4, p5]


def local(
    queries,
    tree_cache,
    tree_mask,
    dest_group,
    accepted_path,
    prompt_cache,
    first_len,
    spill_cache,
    spill_len,
    out_weight,
    *,
    tuned,
):
    req, tree, cols = queries.shape
    prompt = prompt_cache.shape[2]
    padded = (prompt // 16 + 1) * 16
    group = dest_group[:, 0]
    partner = jnp.bitwise_xor(group, 1)
    lens = jnp.stack([first_len[0], spill_len[0]]).astype(jnp.bfloat16)
    bias = jnp.pad(jnp.where(tree_mask == 1, 0.0, NEG_FILL), ((0, 0), (0, 0), (2 * padded, 0)))
    if tuned:
        base = lax.axis_index("rep").astype(jnp.int32)
    else:
        base = jnp.zeros((), jnp.int32)
    idx = jnp.stack([jnp.bitwise_xor(group, base), jnp.bitwise_xor(partner, base)])
    accepted_cache = jnp.take_along_axis(tree_cache, accepted_path[:, None, :, None], axis=2)

    if not tuned:
        block = cache_block(prompt_cache, spill_cache, lens, 0, cols, padded)
        caches = [lax.all_gather(block, "rep", axis=0, tiled=True)]
        attn = attend(idx, queries, tree_cache, bias, caches, 0, cols).reshape(req * tree, cols)
        whole = lax.all_gather(attn, "tp", axis=1, tiled=True)
        summed = jnp.dot(whole, out_weight, preferred_element_type=jnp.float32)
        return summed.astype(jnp.bfloat16).reshape(req, tree, out_weight.shape[1]), accepted_cache

    z = lax.axis_index("tp").astype(jnp.int32).reshape(1)
    weight = out_weight.reshape(lax.axis_size("tp"), cols, out_weight.shape[1])
    chunks = []
    start = 0
    for heads in (1, 1, 2, 2, 2):
        chunks.append((start, heads * HD))
        start += heads * HD
    acc = None
    for i, (start, width) in enumerate(chunks):
        block = cache_block(prompt_cache, spill_cache, lens, start, width, padded)
        caches = gather_caches(block)
        attn = attend(idx, queries, tree_cache, bias, caches, start, width).reshape(req * tree, width)
        pieces = exchange(attn)
        acc = project(z, pieces, weight, acc, start, width, i == len(chunks) - 1)
    return acc.reshape(req, tree, out_weight.shape[1]), accepted_cache


def solution(mesh):
    heads_here = 32 // mesh.shape["tp"]
    tuned = mesh.shape["rep"] == 8 and mesh.shape["tp"] == 4 and heads_here == 8
    return jax.shard_map(
        partial(local, tuned=tuned),
        mesh=mesh,
        in_specs=(
            P("rep", None, "tp"),
            P("rep", None, None, "tp"),
            P("rep", None, None),
            P("rep", None),
            P("rep", None),
            P("rep", None, None, "tp"),
            P("rep"),
            P("rep", None, None, "tp"),
            P("rep"),
            P(None, "tp"),
        ),
        out_specs=(P("rep", None, "tp"), P("rep", None, None, "tp")),
        check_vma=False,
    )
```

```python
import math
from functools import partial

import jax
import jax.numpy as jnp
from jax import lax
from jax.experimental import pallas as pl
from jax.experimental.pallas import tpu as pltpu
from jax.sharding import PartitionSpec as P

HD = 128
NEG_FILL = -1e30
HEAD_CHUNKS = (1, 1, 2, 2, 2)


K_FLOPS = 2_700_000_000
J_FLOPS = 2_000_000_000
GATE = (1, 1, 1)


def cost(flops):
    return pl.CostEstimate(flops=flops, bytes_accessed=1000, transcendentals=0)


SCALE = 1.0 / math.sqrt(HD)
VMEM_BYTES = 6 * 1024 * 1024


def attend_kernel(idx_ref, q_ref, tree_ref, bias_ref, *rest, n_caches):
    cache_refs = rest[:n_caches]
    out_ref, held, sems = rest[n_caches:]
    copies = []
    at = 0
    for i, ref in enumerate(cache_refs):
        size = ref.shape[0]
        copies.append(pltpu.make_async_copy(ref, held.at[pl.ds(at, size)], sems.at[i]))
        at += size
    for copy in copies:
        copy.start()
    for copy in copies:
        copy.wait()
    requests, _, width = q_ref.shape
    padded = held.shape[3]
    n_keys = bias_ref.shape[2]
    position = lax.broadcasted_iota(jnp.int32, (1, n_keys), 1).astype(jnp.float32)
    repeats = -(-n_keys // HD)

    def length_row(block, part):
        tail = held[block, part, 0, pl.ds(padded - 16, 16), 0:HD].astype(jnp.float32)[15:16]
        return jnp.concatenate([tail] * repeats, axis=1)[:, :n_keys]

    def body(r, carry):
        first = idx_ref[0, r]
        second = idx_ref[1, r]
        limit = jnp.where(position < padded, length_row(first, 0), length_row(second, 1) + padded)
        limit = jnp.where(position < 2 * padded, limit, n_keys)
        bias = bias_ref[r] + jnp.where(position < limit, 0.0, NEG_FILL)
        for h in range(width // HD):
            cols = slice(h * HD, (h + 1) * HD)
            keys = jnp.concatenate(
                [held[first, 0, 0, :, cols], held[second, 1, 0, :, cols], tree_ref[r, 0, :, cols]], axis=0
            )
            values = jnp.concatenate(
                [held[first, 0, 1, :, cols], held[second, 1, 1, :, cols], tree_ref[r, 1, :, cols]], axis=0
            )
            scores = lax.dot_general(
                q_ref[r, :, cols], keys, (((1,), (1,)), ((), ())), preferred_element_type=jnp.float32
            )
            scores = scores * SCALE + bias
            raw = jnp.exp(scores - jnp.max(scores, axis=1, keepdims=True))
            total = jnp.sum(raw, axis=1, keepdims=True)
            accum = jnp.dot(raw.astype(jnp.bfloat16), values, preferred_element_type=jnp.float32)
            out_ref[r, :, cols] = (accum / total).astype(out_ref.dtype)
        return carry

    lax.fori_loop(0, requests, body, 0)


def attend(idx, queries, tree_cache, bias, caches, start, width):
    req, tree, _ = queries.shape
    block = start // width
    n_blocks = sum(c.shape[0] for c in caches)
    keys = bias.shape[2]
    return pl.pallas_call(
        partial(attend_kernel, n_caches=len(caches)),
        grid=(1,),
        in_specs=[
            pl.BlockSpec(memory_space=pltpu.SMEM),
            pl.BlockSpec((req, tree, width), lambda i: (0, 0, block)),
            pl.BlockSpec((req, 2, tree, width), lambda i: (0, 0, 0, block)),
            pl.BlockSpec(bias.shape, lambda i: (0, 0, 0)),
        ]
        + [pl.BlockSpec(memory_space=pl.ANY)] * len(caches),
        out_specs=pl.BlockSpec((req, tree, width), lambda i: (0, 0, 0)),
        out_shape=jax.ShapeDtypeStruct((req, tree, width), jnp.bfloat16),
        scratch_shapes=[
            pltpu.VMEM((n_blocks,) + caches[0].shape[1:], jnp.bfloat16),
            pltpu.SemaphoreType.DMA((len(caches),)),
        ],
        compiler_params=pltpu.CompilerParams(vmem_limit_bytes=8 * VMEM_BYTES),
        cost_estimate=pl.CostEstimate(
            flops=4 * req * tree * keys * width * 16, bytes_accessed=8 * n_blocks * 320 * width, transcendentals=0
        ),
    )(idx, queries, tree_cache, bias, *caches)


def paired_kernel(slot_ref, *rest, start, inside, n_caches):
    sides, caches, outs = rest[:6], rest[6 : 6 + n_caches], rest[6 + n_caches :]
    width = outs[0].shape[2]
    tree = outs[0].shape[1]
    padded = caches[0].shape[2]
    n_keys = 2 * tree + 2 * padded
    position = lax.broadcasted_iota(jnp.int32, (1, n_keys), 1).astype(jnp.float32)
    repeats = -(-n_keys // HD)

    def length_row(ref, part):
        tail = ref[part, 0, padded - 16 : padded, 0:HD].astype(jnp.float32)[15:16]
        return jnp.concatenate([tail] * repeats, axis=1)[:, :n_keys]

    lane = lax.broadcasted_iota(jnp.int32, (tree, HD), 1)
    for m, cache in enumerate(caches):
        spill_at = 2 * tree + padded
        limit = jnp.where(position < spill_at, length_row(cache, 0) + 2 * tree, length_row(cache, 1) + spill_at)
        limit = jnp.where(position < 2 * tree, n_keys, limit)
        unseen = jnp.where(position < limit, 0.0, NEG_FILL)
        for side in range(2):
            q_ref, tree_ref, bias_ref = sides[3 * side : 3 * side + 3]
            out_ref = outs[side]
            r0, r1, used = [slot_ref[3 * side + k, m] for k in range(3)]
            used = used > 0
            rolled = jnp.where(lane < tree, NEG_FILL, pltpu.roll(bias_ref[r1], tree, 1))
            rolled = jnp.where(lane < 2 * tree, rolled, 0.0)
            head_bias = jnp.concatenate([bias_ref[r0], rolled], axis=0) + unseen[:, :HD]
            bias = jnp.concatenate(
                [head_bias, jnp.broadcast_to(unseen[:, HD:], (2 * tree, n_keys - HD))], axis=1
            )
            for h in range(width // HD):
                here = slice(h * HD, (h + 1) * HD)
                held = slice(inside + h * HD, inside + (h + 1) * HD)
                cols = slice(start + h * HD, start + (h + 1) * HD)

                def stored(k):
                    return jnp.concatenate(
                        [tree_ref[r0, k, :, cols], tree_ref[r1, k, :, cols], cache[0, k, :, held], cache[1, k, :, held]],
                        axis=0,
                    )

                both = jnp.concatenate([q_ref[r0, :, cols], q_ref[r1, :, cols]], axis=0)
                scores = lax.dot_general(
                    both, stored(0), (((1,), (1,)), ((), ())), preferred_element_type=jnp.float32
                )
                scores = scores * SCALE + bias
                raw = jnp.exp(scores - jnp.max(scores, axis=1, keepdims=True))
                total = jnp.sum(raw, axis=1, keepdims=True)
                accum = jnp.dot(raw.astype(jnp.bfloat16), stored(1), preferred_element_type=jnp.float32)
                attn = (accum / total).astype(out_ref.dtype)
                out_ref[r0, :, here] = jnp.where(used, attn[:tree], out_ref[r0, :, here])
                out_ref[r1, :, here] = jnp.where(used, attn[tree:], out_ref[r1, :, here])


def attend_pairs(slots, sides, caches, start, inside, width):
    req, tree, _ = sides[0].shape
    vmem = pl.BlockSpec(memory_space=pltpu.VMEM)
    return pl.pallas_call(
        partial(paired_kernel, start=start, inside=inside, n_caches=len(caches)),
        in_specs=[pl.BlockSpec(memory_space=pltpu.SMEM)] + [vmem] * (len(sides) + len(caches)),
        out_specs=[vmem, vmem],
        out_shape=[jax.ShapeDtypeStruct((req, tree, width), jnp.bfloat16)] * 2,
        compiler_params=pltpu.CompilerParams(vmem_limit_bytes=VMEM_BYTES),
        cost_estimate=cost(K_FLOPS + K_FLOPS * width // HD),
    )(slots, *sides, *caches)


def project_kernel(z_ref, w_hbm, *rest, parts, counts):
    has_own, has_middle, has_acc = counts
    rest = list(rest)
    own = rest.pop(0) if has_own else None
    outer = rest.pop(0)
    between = rest.pop(0) if has_middle else None
    acc = rest.pop(0) if has_acc else None
    out_ref, w_ref, sems = rest
    z = z_ref[0]
    lower = z < 2
    sources = (z, jnp.bitwise_xor(z, 1), jnp.where(lower, 2, 1), jnp.where(lower, 3, 0))
    tile = w_ref.shape[2]
    tiles = w_ref.shape[0]
    copies = []
    for n in range(tiles):
        at = 0
        for which, start, width in parts:
            copies.append(
                pltpu.make_async_copy(
                    w_hbm.at[sources[which], pl.ds(start, width), pl.ds(n * tile, tile)],
                    w_ref.at[n, pl.ds(at, width), :],
                    sems.at[len(copies)],
                )
            )
            at += width
    for copy in copies:
        copy.start()
    pieces = [own[...]] if has_own else []
    fresh = own.shape[1] if has_own else 0
    if has_own:
        pieces.append(outer[:, :fresh])
    if has_middle:
        middle = jnp.logical_and(z > 0, z < 3)
        pieces.append(jnp.where(middle, between[...], outer[:, fresh:]))
    attn = jnp.concatenate(pieces, axis=1)
    for n in range(tiles):
        for copy in copies[n * len(parts) : (n + 1) * len(parts)]:
            copy.wait()
        cols = slice(n * tile, (n + 1) * tile)
        total = jnp.dot(attn, w_ref[n], preferred_element_type=jnp.float32)
        if has_acc:
            total += acc[:, cols]
        out_ref[:, cols] = total.astype(out_ref.dtype)


def project(z, weight, own, outer, between, acc, parts, last):
    _, _, cols = weight.shape
    rows = outer.shape[0]
    depth = sum(width for _, _, width in parts)
    tile = 256
    tiles = cols // tile
    given = [v for v in (own, outer, between, acc) if v is not None]
    in_place = {1 + len(given): 0} if acc is not None and not last else {}
    vmem = pl.BlockSpec(memory_space=pltpu.VMEM)
    return pl.pallas_call(
        partial(
            project_kernel, parts=parts, counts=(own is not None, between is not None, acc is not None)
        ),
        in_specs=[pl.BlockSpec(memory_space=pltpu.SMEM), pl.BlockSpec(memory_space=pltpu.HBM)] + [vmem] * len(given),
        out_specs=vmem,
        out_shape=jax.ShapeDtypeStruct((rows, cols), jnp.bfloat16 if last else jnp.float32),
        scratch_shapes=[
            pltpu.VMEM((tiles, depth, tile), jnp.bfloat16),
            pltpu.SemaphoreType.DMA((tiles * len(parts),)),
        ],
        input_output_aliases=in_place,
        compiler_params=pltpu.CompilerParams(vmem_limit_bytes=VMEM_BYTES),
        cost_estimate=cost(J_FLOPS),
    )(z, weight, *given)


def cache_block(prompt, spill, lens, start, width, padded):
    both = jnp.stack([prompt[0, ..., start : start + width], spill[0, ..., start : start + width]])
    both = jnp.pad(both, ((0, 0), (0, 0), (0, padded - both.shape[2]), (0, 0)))
    row = lax.broadcasted_iota(jnp.int32, both.shape, 2)
    return jnp.where(row == padded - 1, lens[:, None, None, None], both)


def across(value, mask):
    return lax.ppermute(value, "rep", [(i, i ^ mask) for i in range(lax.axis_size("rep"))])


def along(value, pairs):
    return lax.ppermute(value, "tp", pairs)


def after(value, *earlier):
    return lax.optimization_barrier((value, *earlier))[0]


def pair_slots(group, blocks):
    match = blocks[:, None] == group[None, :]
    order = jnp.arange(group.shape[0], dtype=jnp.int32)[None, :]
    lowest = jnp.min(jnp.where(match, order, group.shape[0]), axis=1)
    highest = jnp.max(jnp.where(match, order, -1), axis=1)
    used = highest >= 0
    return [jnp.where(used, lowest, 0), jnp.where(used, highest, 0), used.astype(jnp.int32)]


def pair_bias(tree_mask):
    bias = jnp.where(tree_mask == 1, 0.0, NEG_FILL).astype(jnp.float32)
    tree = bias.shape[1]
    bias = jnp.pad(bias, ((0, 0), (0, 0), (0, tree)), constant_values=NEG_FILL)
    return jnp.pad(bias, ((0, 0), (0, 0), (0, HD - 2 * tree)))


def local(
    queries,
    tree_cache,
    tree_mask,
    dest_group,
    accepted_path,
    prompt_cache,
    first_len,
    spill_cache,
    spill_len,
    out_weight,
    *,
    tuned,
):
    req, tree, cols = queries.shape
    prompt = prompt_cache.shape[2]
    padded = (prompt // 16 + 1) * 16
    group = dest_group[:, 0]

    if not tuned:
        accepted_cache = jnp.take_along_axis(tree_cache, accepted_path[:, None, :, None], axis=2)
        lens = jnp.stack([first_len[0], spill_len[0]]).astype(jnp.bfloat16)
        idx = jnp.stack([group, jnp.bitwise_xor(group, 1)])
        bias = jnp.where(tree_mask == 1, 0.0, NEG_FILL).astype(jnp.float32)
        bias = jnp.pad(bias, ((0, 0), (0, 0), (2 * padded, 0)))
        block = cache_block(prompt_cache, spill_cache, lens, 0, cols, padded)
        caches = lax.all_gather(block, "rep", axis=0, tiled=False)
        attn = attend(idx, queries, tree_cache, bias, [caches], 0, cols).reshape(req * tree, cols)
        whole = lax.all_gather(attn, "tp", axis=1, tiled=True)
        summed = jnp.dot(whole, out_weight, preferred_element_type=jnp.float32)
        return summed.astype(jnp.bfloat16).reshape(req, tree, out_weight.shape[1]), accepted_cache

    spill = across(spill_cache, 1)
    lens = jnp.stack([first_len[0], across(spill_len, 1)[0]]).astype(jnp.bfloat16)
    other_queries = across(queries, 1)
    other_tree = across(tree_cache, 1)
    other_mask = across(tree_mask, 1)
    other_group = across(dest_group, 1)

    chunks = []
    start = 0
    for heads in HEAD_CHUNKS:
        chunks.append((start, heads * HD))
        start += heads * HD
    n = len(chunks)
    gathered, owns, raws = [], [], []

    def gather(i):
        start, width = chunks[i]
        block = cache_block(prompt_cache, spill, lens, start, width, padded)
        if i > 0:
            block = after(block, *gathered[i - 1][1:], *raws[max(i - 2, 0) : i - 1])
        gathered.append([block] + [across(block, m) for m in (2, 4, 6)])

    gather(0)
    group, other_group, tree_mask, other_mask = lax.optimization_barrier(
        (group, other_group[:, 0], tree_mask, other_mask, gathered[0][0])
    )[:4]
    me = lax.axis_index("rep").astype(jnp.int32)
    blocks = jnp.bitwise_xor(me, jnp.array([0, 2, 4, 6], jnp.int32))
    slots = jnp.stack(pair_slots(group, blocks) + pair_slots(other_group, blocks))
    sides = [queries, tree_cache, pair_bias(tree_mask), other_queries, other_tree, pair_bias(other_mask)]
    mine = jnp.bitwise_and(jnp.bitwise_xor(group, me), 1) == 0

    z = lax.axis_index("tp").astype(jnp.int32).reshape(1)
    weight = out_weight.reshape(lax.axis_size("tp"), cols, out_weight.shape[1])
    acc = None
    accs, outer, between = [], [], []
    for i in range(n + 2):
        fresh = []
        if i < n:
            start, width = chunks[i]
            ready = slots
            if i > 0:
                gates = [owns[i - 1]] + between[max(i - 2, 0) : i - 1] + accs[max(i - 3, 0) : i - 2]
                ready = after(slots, *gates)
            own, theirs = attend_pairs(ready, sides, gathered[i], start, 0, width)
            raws.append(theirs)
            if i + 1 < n:
                gather(i + 1)
                if GATE[0]:
                    theirs = after(theirs, *gathered[i + 1][1:])
            if i > 0 and GATE[1]:
                theirs = after(theirs, between[i - 1])
            if i > 0 and GATE[2]:
                theirs = after(theirs, outer[i - 1])
            attn = jnp.where(mine[:, None, None], own, across(theirs, 1)).reshape(req * tree, width)
            owns.append(attn)
            fresh = [attn]
        payload = fresh + ([between[i - 1]] if i > 0 else [])
        payload = jnp.concatenate(payload, axis=1)
        if i > 1:
            payload = after(payload, accs[i - 2])
        outer.append(along(payload, [(0, 1), (1, 0), (2, 3), (3, 2)] if i < n else [(1, 0), (2, 3)]))
        if i <= n:
            relayed = [outer[i - 1][:, : chunks[i - 1][1]]] if i > 0 else []
            between.append(along(jnp.concatenate(fresh + relayed, axis=1), [(1, 2), (2, 1)]))
        parts = [(0, *chunks[i]), (1, *chunks[i])] if i < n else []
        parts += [(2, *chunks[i - 1])] if 0 < i <= n else []
        parts += [(3, *chunks[i - 2])] if i > 1 else []
        acc = project(
            z, weight, owns[i] if i < n else None, outer[i], between[i - 1] if i > 0 else None, acc, parts, i == n + 1
        )
        accs.append(acc)
    path = after(accepted_path, owns[-1])
    accepted_cache = jnp.take_along_axis(tree_cache, path[:, None, :, None], axis=2)
    return acc.reshape(req, tree, out_weight.shape[1]), accepted_cache


def solution(mesh):
    heads_here = 32 // mesh.shape["tp"]
    tuned = mesh.shape["rep"] == 8 and mesh.shape["tp"] == 4 and heads_here == sum(HEAD_CHUNKS)
    return jax.shard_map(
        partial(local, tuned=tuned),
        mesh=mesh,
        in_specs=(
            P("rep", None, "tp"),
            P("rep", None, None, "tp"),
            P("rep", None, None),
            P("rep", None),
            P("rep", None),
            P("rep", None, None, "tp"),
            P("rep"),
            P("rep", None, None, "tp"),
            P("rep"),
            P(None, "tp"),
        ),
        out_specs=(P("rep", None, "tp"), P("rep", None, None, "tp")),
        check_vma=False,
    )
```

```python
import math
from functools import partial

import jax
import jax.numpy as jnp
from jax import lax
from jax.experimental import pallas as pl
from jax.experimental.pallas import tpu as pltpu
from jax.sharding import PartitionSpec as P

HD = 128
NEG_FILL = -1e30
HEAD_CHUNKS = (2, 2, 2, 2)
SPLITS = (2, 3, 4, 5)


K_FLOPS = 2_700_000_000
J_FLOPS = 2_000_000_000
GATE = (0, 1, 1)


def cost(flops):
    return pl.CostEstimate(flops=flops, bytes_accessed=1000, transcendentals=0)


SCALE = 1.0 / math.sqrt(HD)
LOG2E = math.log2(math.e)
VMEM_BYTES = 10 * 1024 * 1024
J_VMEM = 12 * 1024 * 1024


def attend_kernel(idx_ref, q_ref, tree_ref, bias_ref, *rest, n_caches):
    cache_refs = rest[:n_caches]
    out_ref, held, sems = rest[n_caches:]
    copies = []
    at = 0
    for i, ref in enumerate(cache_refs):
        size = ref.shape[0]
        copies.append(pltpu.make_async_copy(ref, held.at[pl.ds(at, size)], sems.at[i]))
        at += size
    for copy in copies:
        copy.start()
    for copy in copies:
        copy.wait()
    requests, _, width = q_ref.shape
    padded = held.shape[3]
    n_keys = bias_ref.shape[2]
    position = lax.broadcasted_iota(jnp.int32, (1, n_keys), 1).astype(jnp.float32)
    repeats = -(-n_keys // HD)

    def length_row(block, part):
        tail = held[block, part, 0, pl.ds(padded - 16, 16), 0:HD].astype(jnp.float32)[15:16]
        return jnp.concatenate([tail] * repeats, axis=1)[:, :n_keys]

    def body(r, carry):
        first = idx_ref[0, r]
        second = idx_ref[1, r]
        limit = jnp.where(position < padded, length_row(first, 0), length_row(second, 1) + padded)
        limit = jnp.where(position < 2 * padded, limit, n_keys)
        bias = bias_ref[r] + jnp.where(position < limit, 0.0, NEG_FILL)
        for h in range(width // HD):
            cols = slice(h * HD, (h + 1) * HD)
            keys = jnp.concatenate(
                [held[first, 0, 0, :, cols], held[second, 1, 0, :, cols], tree_ref[r, 0, :, cols]], axis=0
            )
            values = jnp.concatenate(
                [held[first, 0, 1, :, cols], held[second, 1, 1, :, cols], tree_ref[r, 1, :, cols]], axis=0
            )
            scores = lax.dot_general(
                q_ref[r, :, cols], keys, (((1,), (1,)), ((), ())), preferred_element_type=jnp.float32
            )
            scores = scores * SCALE + bias
            raw = jnp.exp(scores - jnp.max(scores, axis=1, keepdims=True))
            total = jnp.sum(raw, axis=1, keepdims=True)
            accum = jnp.dot(raw.astype(jnp.bfloat16), values, preferred_element_type=jnp.float32)
            out_ref[r, :, cols] = (accum / total).astype(out_ref.dtype)
        return carry

    lax.fori_loop(0, requests, body, 0)


def attend(idx, queries, tree_cache, bias, caches, start, width):
    req, tree, _ = queries.shape
    block = start // width
    n_blocks = sum(c.shape[0] for c in caches)
    keys = bias.shape[2]
    return pl.pallas_call(
        partial(attend_kernel, n_caches=len(caches)),
        grid=(1,),
        in_specs=[
            pl.BlockSpec(memory_space=pltpu.SMEM),
            pl.BlockSpec((req, tree, width), lambda i: (0, 0, block)),
            pl.BlockSpec((req, 2, tree, width), lambda i: (0, 0, 0, block)),
            pl.BlockSpec(bias.shape, lambda i: (0, 0, 0)),
        ]
        + [pl.BlockSpec(memory_space=pl.ANY)] * len(caches),
        out_specs=pl.BlockSpec((req, tree, width), lambda i: (0, 0, 0)),
        out_shape=jax.ShapeDtypeStruct((req, tree, width), jnp.bfloat16),
        scratch_shapes=[
            pltpu.VMEM((n_blocks,) + caches[0].shape[1:], jnp.bfloat16),
            pltpu.SemaphoreType.DMA((len(caches),)),
        ],
        compiler_params=pltpu.CompilerParams(vmem_limit_bytes=8 * VMEM_BYTES),
        cost_estimate=pl.CostEstimate(
            flops=4 * req * tree * keys * width * 16, bytes_accessed=8 * n_blocks * 320 * width, transcendentals=0
        ),
    )(idx, queries, tree_cache, bias, *caches)


def paired_kernel(slot_ref, *rest, start, inside, n_caches):
    sides, caches, outs = rest[:6], rest[6 : 6 + n_caches], rest[6 + n_caches :]
    width = outs[0].shape[2]
    tree = outs[0].shape[1]
    padded = caches[0].shape[2]
    own_keys = 4 * tree
    n_keys = own_keys + 2 * padded
    spill_at = own_keys + padded
    lanes = sides[2].shape[2]
    position = lax.broadcasted_iota(jnp.int32, (1, n_keys), 1).astype(jnp.float32)
    lane = lax.broadcasted_iota(jnp.int32, (tree, lanes), 1)
    repeats = -(-n_keys // HD)

    def length_row(ref, part):
        tail = ref[part, 0, padded - 16 : padded, 0:HD].astype(jnp.float32)[15:16]
        return jnp.concatenate([tail] * repeats, axis=1)[:, :n_keys]

    for m, cache in enumerate(caches):
        limit = jnp.where(position < spill_at, length_row(cache, 0) + own_keys, length_row(cache, 1) + spill_at)
        limit = jnp.where(position < own_keys, n_keys, limit)
        unseen = jnp.where(position < limit, 0.0, NEG_FILL)
        rows, used = [], []
        for side in range(2):
            for k in range(2):
                rows.append((side, slot_ref[3 * side + k, m]))
                used.append(slot_ref[3 * side + 2, m] > 0)
        head_bias = []
        for i, (side, r) in enumerate(rows):
            block = sides[3 * side + 2][r]
            block = block if i == 0 else pltpu.roll(block, i * tree, 1)
            here = jnp.logical_and(lane >= i * tree, lane < (i + 1) * tree)
            head_bias.append(jnp.where(here, block, jnp.where(lane < own_keys, NEG_FILL, 0.0)))
        bias = jnp.concatenate(
            [
                jnp.concatenate(head_bias, axis=0) + unseen[:, :lanes],
                jnp.broadcast_to(unseen[:, lanes:], (own_keys, n_keys - lanes)),
            ],
            axis=1,
        )
        results = []
        for h in range(width // HD):
            here = slice(h * HD, (h + 1) * HD)
            held = slice(inside + h * HD, inside + (h + 1) * HD)
            cols = slice(start + h * HD, start + (h + 1) * HD)

            def stored(k):
                own = [sides[3 * side + 1][r, k, :, cols] for side, r in rows]
                return jnp.concatenate(own + [cache[0, k, :, held], cache[1, k, :, held]], axis=0)

            asked = jnp.concatenate([sides[3 * side][r, :, cols] for side, r in rows], axis=0)
            scores = lax.dot_general(
                asked, stored(0), (((1,), (1,)), ((), ())), preferred_element_type=jnp.float32
            )
            scores = scores * (SCALE * LOG2E) + bias
            raw = jnp.exp2(scores - jnp.max(scores, axis=1, keepdims=True))
            total = jnp.sum(raw, axis=1, keepdims=True)
            accum = jnp.dot(raw.astype(jnp.bfloat16), stored(1), preferred_element_type=jnp.float32)
            results.append((here, (accum / total).astype(jnp.bfloat16)))
        for here, attn in results:
            for i, (side, r) in enumerate(rows):
                mine = attn[i * tree : (i + 1) * tree]
                outs[side][r, :, here] = jnp.where(used[i], mine, outs[side][r, :, here])


def attend_pairs(slots, sides, caches, start, inside, width):
    req, tree, _ = sides[0].shape
    vmem = pl.BlockSpec(memory_space=pltpu.VMEM)
    return pl.pallas_call(
        partial(paired_kernel, start=start, inside=inside, n_caches=len(caches)),
        in_specs=[pl.BlockSpec(memory_space=pltpu.SMEM)] + [vmem] * (len(sides) + len(caches)),
        out_specs=[vmem, vmem],
        out_shape=[jax.ShapeDtypeStruct((req, tree, width), jnp.bfloat16)] * 2,
        compiler_params=pltpu.CompilerParams(vmem_limit_bytes=VMEM_BYTES),
        cost_estimate=cost(K_FLOPS + K_FLOPS * width // HD),
    )(slots, *sides, *caches)


def project_kernel(z_ref, w_hbm, *rest, steps, has_acc):
    rest = list(rest)
    acc = rest.pop(0) if has_acc else None
    out_ref, w_ref, sems = rest[-3:]
    z = z_ref[0]
    lower = z < 2
    middle = jnp.logical_and(z > 0, z < 3)
    sources = (z, jnp.bitwise_xor(z, 1), jnp.where(lower, 2, 1), jnp.where(lower, 3, 0))
    copies = []
    at = 0
    for _, _, step in steps:
        for which, start, width in step:
            copies.append(
                pltpu.make_async_copy(
                    w_hbm.at[sources[which], pl.ds(start, width), :],
                    w_ref.at[pl.ds(at, width), :],
                    sems.at[len(copies)],
                )
            )
            copies[-1].start()
            at += width
    pieces = []
    for has_own, has_middle, _ in steps:
        own = rest.pop(0) if has_own else None
        outer = rest.pop(0)
        fresh = own.shape[1] if has_own else 0
        if has_own:
            pieces += [own[...], outer[:, :fresh]]
        if has_middle:
            pieces.append(jnp.where(middle, rest.pop(0)[...], outer[:, fresh:]))
    attn = jnp.concatenate(pieces, axis=1)
    for copy in copies:
        copy.wait()
    tile = 256
    for n in range(out_ref.shape[1] // tile):
        cols = slice(n * tile, (n + 1) * tile)
        total = jnp.dot(attn, w_ref[:, cols], preferred_element_type=jnp.float32)
        if has_acc:
            total += acc[:, cols]
        out_ref[:, cols] = total.astype(out_ref.dtype)


def project(z, weight, steps, acc, last):
    _, _, cols = weight.shape
    given = [] if acc is None else [acc]
    shape = []
    for own, outer, between, parts in steps:
        given += [v for v in (own, outer, between) if v is not None]
        shape.append((own is not None, between is not None, tuple(parts)))
    count = sum(len(step[2]) for step in shape)
    depth = sum(width for step in shape for _, _, width in step[2])
    rows = steps[0][1].shape[0]
    vmem = pl.BlockSpec(memory_space=pltpu.VMEM)
    return pl.pallas_call(
        partial(project_kernel, steps=tuple(shape), has_acc=acc is not None),
        in_specs=[pl.BlockSpec(memory_space=pltpu.SMEM), pl.BlockSpec(memory_space=pltpu.HBM)] + [vmem] * len(given),
        out_specs=vmem,
        out_shape=jax.ShapeDtypeStruct((rows, cols), jnp.bfloat16 if last else jnp.float32),
        scratch_shapes=[
            pltpu.VMEM((depth, cols), jnp.bfloat16),
            pltpu.SemaphoreType.DMA((count,)),
        ],
        input_output_aliases={2: 0} if acc is not None and not last else {},
        compiler_params=pltpu.CompilerParams(vmem_limit_bytes=J_VMEM),
        cost_estimate=cost(J_FLOPS),
    )(z, weight, *given)


def cache_block(prompt, spill, lens, start, width, padded):
    both = jnp.stack([prompt[0, ..., start : start + width], spill[0, ..., start : start + width]])
    both = jnp.pad(both, ((0, 0), (0, 0), (0, padded - both.shape[2]), (0, 0)))
    row = lax.broadcasted_iota(jnp.int32, both.shape, 2)
    return jnp.where(row == padded - 1, lens[:, None, None, None], both)


def across(value, mask):
    return lax.ppermute(value, "rep", [(i, i ^ mask) for i in range(lax.axis_size("rep"))])


def along(value, pairs):
    return lax.ppermute(value, "tp", pairs)


def after(value, *earlier):
    return lax.optimization_barrier((value, *earlier))[0]


def pair_slots(group, blocks):
    match = blocks[:, None] == group[None, :]
    order = jnp.arange(group.shape[0], dtype=jnp.int32)[None, :]
    lowest = jnp.min(jnp.where(match, order, group.shape[0]), axis=1)
    highest = jnp.max(jnp.where(match, order, -1), axis=1)
    used = highest >= 0
    return [jnp.where(used, lowest, 0), jnp.where(used, highest, 0), used.astype(jnp.int32)]


def pair_bias(tree_mask):
    bias = jnp.where(tree_mask == 1, 0.0, NEG_FILL).astype(jnp.float32)
    tree = bias.shape[1]
    return jnp.pad(bias, ((0, 0), (0, 0), (0, -(-4 * tree // HD) * HD - tree)))


def local(
    queries,
    tree_cache,
    tree_mask,
    dest_group,
    accepted_path,
    prompt_cache,
    first_len,
    spill_cache,
    spill_len,
    out_weight,
    *,
    tuned,
):
    req, tree, cols = queries.shape
    prompt = prompt_cache.shape[2]
    padded = (prompt // 16 + 1) * 16
    group = dest_group[:, 0]

    if not tuned:
        accepted_cache = jnp.take_along_axis(tree_cache, accepted_path[:, None, :, None], axis=2)
        lens = jnp.stack([first_len[0], spill_len[0]]).astype(jnp.bfloat16)
        idx = jnp.stack([group, jnp.bitwise_xor(group, 1)])
        bias = jnp.where(tree_mask == 1, 0.0, NEG_FILL).astype(jnp.float32)
        bias = jnp.pad(bias, ((0, 0), (0, 0), (2 * padded, 0)))
        block = cache_block(prompt_cache, spill_cache, lens, 0, cols, padded)
        caches = lax.all_gather(block, "rep", axis=0, tiled=False)
        attn = attend(idx, queries, tree_cache, bias, [caches], 0, cols).reshape(req * tree, cols)
        whole = lax.all_gather(attn, "tp", axis=1, tiled=True)
        summed = jnp.dot(whole, out_weight, preferred_element_type=jnp.float32)
        return summed.astype(jnp.bfloat16).reshape(req, tree, out_weight.shape[1]), accepted_cache

    spill = across(spill_cache, 1)
    lens = jnp.stack([first_len[0], across(spill_len, 1)[0]]).astype(jnp.bfloat16)
    chunks = []
    start = 0
    for heads in HEAD_CHUNKS:
        chunks.append((start, heads * HD))
        start += heads * HD
    n = len(chunks)
    gathered, owns, raws = [], [], []

    def gather(i):
        start, width = chunks[i]
        block = cache_block(prompt_cache, spill, lens, start, width, padded)
        if i > 0:
            block = after(block, *gathered[i - 1][1:], *raws[max(i - 2, 0) : i - 1])
        gathered.append([block] + [across(block, m) for m in (2, 4, 6)])

    gather(0)
    queries, tree_cache, tree_mask, dest_group = lax.optimization_barrier(
        (queries, tree_cache, tree_mask, dest_group, gathered[0][0])
    )[:4]
    other_queries = across(queries, 1)
    other_tree = across(tree_cache, 1)
    other_mask = across(tree_mask, 1)
    group, other_group = dest_group[:, 0], across(dest_group, 1)[:, 0]
    me = lax.axis_index("rep").astype(jnp.int32)
    blocks = jnp.bitwise_xor(me, jnp.array([0, 2, 4, 6], jnp.int32))
    slots = jnp.stack(pair_slots(group, blocks) + pair_slots(other_group, blocks))
    sides = [queries, tree_cache, pair_bias(tree_mask), other_queries, other_tree, pair_bias(other_mask)]
    mine = jnp.bitwise_and(jnp.bitwise_xor(group, me), 1) == 0

    z = lax.axis_index("tp").astype(jnp.int32).reshape(1)
    weight = out_weight.reshape(lax.axis_size("tp"), cols, out_weight.shape[1])
    acc = None
    steps, outer, between = [], [], []
    for i in range(n + 2):
        fresh = []
        if i < n:
            start, width = chunks[i]
            ready = slots
            if i > 0:
                gates = [owns[i - 1]] + between[max(i - 2, 0) : i - 1]
                ready = after(slots, *gates)
            own, theirs = attend_pairs(ready, sides, gathered[i], start, 0, width)
            raws.append(theirs)
            if i + 1 < n:
                gather(i + 1)
                if GATE[0] == 1 or i > 0 and GATE[0] == 2:
                    theirs = after(theirs, *gathered[i + 1][1:])
            if i > 0 and GATE[1]:
                theirs = after(theirs, between[i - 1])
            if i > 0 and (GATE[2] == 1 or i < n - 1 and GATE[2] == 2 or i == 1 and GATE[2] == 3):
                theirs = after(theirs, outer[i - 1])
            attn = jnp.where(mine[:, None, None], own, across(theirs, 1)).reshape(req * tree, width)
            owns.append(attn)
            fresh = [attn]
        payload = fresh + ([between[i - 1]] if i > 0 else [])
        payload = jnp.concatenate(payload, axis=1)
        outer.append(along(payload, [(0, 1), (1, 0), (2, 3), (3, 2)] if i < n else [(1, 0), (2, 3)]))
        if i <= n:
            relayed = [outer[i - 1][:, : chunks[i - 1][1]]] if i > 0 else []
            between.append(along(jnp.concatenate(fresh + relayed, axis=1), [(1, 2), (2, 1)]))
        parts = [(0, *chunks[i]), (1, *chunks[i])] if i < n else []
        parts += [(2, *chunks[i - 1])] if 0 < i <= n else []
        parts += [(3, *chunks[i - 2])] if i > 1 else []
        steps.append(
            (owns[i] if i < n else None, outer[i], between[i - 1] if i > 0 else None, parts)
        )
        if i in SPLITS:
            acc = project(after(z, raws[-1]), weight, steps, acc, i == n + 1)
            steps = []
    path = after(accepted_path, owns[-1])
    accepted_cache = jnp.take_along_axis(tree_cache, path[:, None, :, None], axis=2)
    return acc.reshape(req, tree, out_weight.shape[1]), accepted_cache


def solution(mesh):
    heads_here = 32 // mesh.shape["tp"]
    tuned = mesh.shape["rep"] == 8 and mesh.shape["tp"] == 4 and heads_here == sum(HEAD_CHUNKS)
    return jax.shard_map(
        partial(local, tuned=tuned),
        mesh=mesh,
        in_specs=(
            P("rep", None, "tp"),
            P("rep", None, None, "tp"),
            P("rep", None, None),
            P("rep", None),
            P("rep", None),
            P("rep", None, None, "tp"),
            P("rep"),
            P("rep", None, None, "tp"),
            P("rep"),
            P(None, "tp"),
        ),
        out_specs=(P("rep", None, "tp"), P("rep", None, None, "tp")),
        check_vma=False,
    )
```

```python
import math
from functools import partial

import jax
import jax.numpy as jnp
from jax import lax
from jax.experimental import pallas as pl
from jax.experimental.pallas import tpu as pltpu
from jax.sharding import PartitionSpec as P

HD = 128
NEG_FILL = -1e30
HEAD_CHUNKS = (2, 2, 2, 2)
SPLITS = (2, 3, 4, 5)
FRONT = 1


K_FLOPS = 2_700_000_000
J_FLOPS = 2_000_000_000
GATE = (0, 1, 1)


def cost(flops):
    return pl.CostEstimate(flops=flops, bytes_accessed=1000, transcendentals=0)


SCALE = 1.0 / math.sqrt(HD)
LOG2E = math.log2(math.e)
VMEM_BYTES = 10 * 1024 * 1024
J_VMEM = 12 * 1024 * 1024


def attend_kernel(idx_ref, q_ref, tree_ref, bias_ref, *rest, n_caches):
    cache_refs = rest[:n_caches]
    out_ref, held, sems = rest[n_caches:]
    copies = []
    at = 0
    for i, ref in enumerate(cache_refs):
        size = ref.shape[0]
        copies.append(pltpu.make_async_copy(ref, held.at[pl.ds(at, size)], sems.at[i]))
        at += size
    for copy in copies:
        copy.start()
    for copy in copies:
        copy.wait()
    requests, _, width = q_ref.shape
    padded = held.shape[3]
    n_keys = bias_ref.shape[2]
    position = lax.broadcasted_iota(jnp.int32, (1, n_keys), 1).astype(jnp.float32)
    repeats = -(-n_keys // HD)

    def length_row(block, part):
        tail = held[block, part, 0, pl.ds(padded - 16, 16), 0:HD].astype(jnp.float32)[15:16]
        return jnp.concatenate([tail] * repeats, axis=1)[:, :n_keys]

    def body(r, carry):
        first = idx_ref[0, r]
        second = idx_ref[1, r]
        limit = jnp.where(position < padded, length_row(first, 0), length_row(second, 1) + padded)
        limit = jnp.where(position < 2 * padded, limit, n_keys)
        bias = bias_ref[r] + jnp.where(position < limit, 0.0, NEG_FILL)
        for h in range(width // HD):
            cols = slice(h * HD, (h + 1) * HD)
            keys = jnp.concatenate(
                [held[first, 0, 0, :, cols], held[second, 1, 0, :, cols], tree_ref[r, 0, :, cols]], axis=0
            )
            values = jnp.concatenate(
                [held[first, 0, 1, :, cols], held[second, 1, 1, :, cols], tree_ref[r, 1, :, cols]], axis=0
            )
            scores = lax.dot_general(
                q_ref[r, :, cols], keys, (((1,), (1,)), ((), ())), preferred_element_type=jnp.float32
            )
            scores = scores * SCALE + bias
            raw = jnp.exp(scores - jnp.max(scores, axis=1, keepdims=True))
            total = jnp.sum(raw, axis=1, keepdims=True)
            accum = jnp.dot(raw.astype(jnp.bfloat16), values, preferred_element_type=jnp.float32)
            out_ref[r, :, cols] = (accum / total).astype(out_ref.dtype)
        return carry

    lax.fori_loop(0, requests, body, 0)


def attend(idx, queries, tree_cache, bias, caches, start, width):
    req, tree, _ = queries.shape
    block = start // width
    n_blocks = sum(c.shape[0] for c in caches)
    keys = bias.shape[2]
    return pl.pallas_call(
        partial(attend_kernel, n_caches=len(caches)),
        grid=(1,),
        in_specs=[
            pl.BlockSpec(memory_space=pltpu.SMEM),
            pl.BlockSpec((req, tree, width), lambda i: (0, 0, block)),
            pl.BlockSpec((req, 2, tree, width), lambda i: (0, 0, 0, block)),
            pl.BlockSpec(bias.shape, lambda i: (0, 0, 0)),
        ]
        + [pl.BlockSpec(memory_space=pl.ANY)] * len(caches),
        out_specs=pl.BlockSpec((req, tree, width), lambda i: (0, 0, 0)),
        out_shape=jax.ShapeDtypeStruct((req, tree, width), jnp.bfloat16),
        scratch_shapes=[
            pltpu.VMEM((n_blocks,) + caches[0].shape[1:], jnp.bfloat16),
            pltpu.SemaphoreType.DMA((len(caches),)),
        ],
        compiler_params=pltpu.CompilerParams(vmem_limit_bytes=8 * VMEM_BYTES),
        cost_estimate=pl.CostEstimate(
            flops=4 * req * tree * keys * width * 16, bytes_accessed=8 * n_blocks * 320 * width, transcendentals=0
        ),
    )(idx, queries, tree_cache, bias, *caches)


def paired_kernel(slot_ref, *rest, start, inside, n_caches):
    sides, caches, outs = rest[:6], rest[6 : 6 + n_caches], rest[6 + n_caches :]
    width = outs[0].shape[2]
    tree = outs[0].shape[1]
    padded = caches[0].shape[2]
    own_keys = 4 * tree
    n_keys = own_keys + 2 * padded
    spill_at = own_keys + padded
    lanes = sides[2].shape[2]
    position = lax.broadcasted_iota(jnp.int32, (1, n_keys), 1).astype(jnp.float32)
    lane = lax.broadcasted_iota(jnp.int32, (tree, lanes), 1)
    repeats = -(-n_keys // HD)

    def length_row(ref, part):
        tail = ref[part, 0, padded - 16 : padded, 0:HD].astype(jnp.float32)[15:16]
        return jnp.concatenate([tail] * repeats, axis=1)[:, :n_keys]

    for m, cache in enumerate(caches):
        limit = jnp.where(position < spill_at, length_row(cache, 0) + own_keys, length_row(cache, 1) + spill_at)
        limit = jnp.where(position < own_keys, n_keys, limit)
        unseen = jnp.where(position < limit, 0.0, NEG_FILL)
        rows, used = [], []
        for side in range(2):
            for k in range(2):
                rows.append((side, slot_ref[3 * side + k, m]))
                used.append(slot_ref[3 * side + 2, m] > 0)
        head_bias = []
        for i, (side, r) in enumerate(rows):
            block = sides[3 * side + 2][r]
            block = block if i == 0 else pltpu.roll(block, i * tree, 1)
            here = jnp.logical_and(lane >= i * tree, lane < (i + 1) * tree)
            head_bias.append(jnp.where(here, block, jnp.where(lane < own_keys, NEG_FILL, 0.0)))
        bias = jnp.concatenate(
            [
                jnp.concatenate(head_bias, axis=0) + unseen[:, :lanes],
                jnp.broadcast_to(unseen[:, lanes:], (own_keys, n_keys - lanes)),
            ],
            axis=1,
        )
        results = []
        for h in range(width // HD):
            here = slice(h * HD, (h + 1) * HD)
            held = slice(inside + h * HD, inside + (h + 1) * HD)
            cols = slice(start + h * HD, start + (h + 1) * HD)

            def stored(k):
                own = [sides[3 * side + 1][r, k, :, cols] for side, r in rows]
                return jnp.concatenate(own + [cache[0, k, :, held], cache[1, k, :, held]], axis=0)

            asked = jnp.concatenate([sides[3 * side][r, :, cols] for side, r in rows], axis=0)
            scores = lax.dot_general(
                asked, stored(0), (((1,), (1,)), ((), ())), preferred_element_type=jnp.float32
            )
            scores = scores * (SCALE * LOG2E) + bias
            raw = jnp.exp2(scores - jnp.max(scores, axis=1, keepdims=True))
            total = jnp.sum(raw, axis=1, keepdims=True)
            accum = jnp.dot(raw.astype(jnp.bfloat16), stored(1), preferred_element_type=jnp.float32)
            results.append((here, (accum / total).astype(jnp.bfloat16)))
        for here, attn in results:
            for i, (side, r) in enumerate(rows):
                mine = attn[i * tree : (i + 1) * tree]
                outs[side][r, :, here] = jnp.where(used[i], mine, outs[side][r, :, here])


def attend_pairs(slots, sides, caches, start, inside, width):
    req, tree, _ = sides[0].shape
    vmem = pl.BlockSpec(memory_space=pltpu.VMEM)
    return pl.pallas_call(
        partial(paired_kernel, start=start, inside=inside, n_caches=len(caches)),
        in_specs=[pl.BlockSpec(memory_space=pltpu.SMEM)] + [vmem] * (len(sides) + len(caches)),
        out_specs=[vmem, vmem],
        out_shape=[jax.ShapeDtypeStruct((req, tree, width), jnp.bfloat16)] * 2,
        compiler_params=pltpu.CompilerParams(vmem_limit_bytes=VMEM_BYTES),
        cost_estimate=cost(K_FLOPS + K_FLOPS * width // HD),
    )(slots, *sides, *caches)


def project_kernel(z_ref, w_hbm, *rest, steps, has_acc):
    rest = list(rest)
    acc = rest.pop(0) if has_acc else None
    out_ref, w_ref, sems = rest[-3:]
    z = z_ref[0]
    lower = z < 2
    middle = jnp.logical_and(z > 0, z < 3)
    sources = (z, jnp.bitwise_xor(z, 1), jnp.where(lower, 2, 1), jnp.where(lower, 3, 0))
    copies = []
    at = 0
    for _, _, step in steps:
        for which, start, width in step:
            copies.append(
                pltpu.make_async_copy(
                    w_hbm.at[sources[which], pl.ds(start, width), :],
                    w_ref.at[pl.ds(at, width), :],
                    sems.at[len(copies)],
                )
            )
            copies[-1].start()
            at += width
    pieces = []
    for has_own, has_middle, _ in steps:
        own = rest.pop(0) if has_own else None
        outer = rest.pop(0)
        fresh = own.shape[1] if has_own else 0
        if has_own:
            pieces += [own[...], outer[:, :fresh]]
        if has_middle:
            pieces.append(jnp.where(middle, rest.pop(0)[...], outer[:, fresh:]))
    attn = jnp.concatenate(pieces, axis=1)
    for copy in copies:
        copy.wait()
    tile = 256
    for n in range(out_ref.shape[1] // tile):
        cols = slice(n * tile, (n + 1) * tile)
        total = jnp.dot(attn, w_ref[:, cols], preferred_element_type=jnp.float32)
        if has_acc:
            total += acc[:, cols]
        out_ref[:, cols] = total.astype(out_ref.dtype)


def project(z, weight, steps, acc, last):
    _, _, cols = weight.shape
    given = [] if acc is None else [acc]
    shape = []
    for own, outer, between, parts in steps:
        given += [v for v in (own, outer, between) if v is not None]
        shape.append((own is not None, between is not None, tuple(parts)))
    count = sum(len(step[2]) for step in shape)
    depth = sum(width for step in shape for _, _, width in step[2])
    rows = steps[0][1].shape[0]
    vmem = pl.BlockSpec(memory_space=pltpu.VMEM)
    return pl.pallas_call(
        partial(project_kernel, steps=tuple(shape), has_acc=acc is not None),
        in_specs=[pl.BlockSpec(memory_space=pltpu.SMEM), pl.BlockSpec(memory_space=pltpu.HBM)] + [vmem] * len(given),
        out_specs=vmem,
        out_shape=jax.ShapeDtypeStruct((rows, cols), jnp.bfloat16 if last else jnp.float32),
        scratch_shapes=[
            pltpu.VMEM((depth, cols), jnp.bfloat16),
            pltpu.SemaphoreType.DMA((count,)),
        ],
        input_output_aliases={2: 0} if acc is not None and not last else {},
        compiler_params=pltpu.CompilerParams(vmem_limit_bytes=J_VMEM),
        cost_estimate=cost(J_FLOPS),
    )(z, weight, *given)


def cache_block(prompt, spill, lens, start, width, padded):
    both = jnp.stack([prompt[0, ..., start : start + width], spill[0, ..., start : start + width]])
    both = jnp.pad(both, ((0, 0), (0, 0), (0, padded - both.shape[2]), (0, 0)))
    row = lax.broadcasted_iota(jnp.int32, both.shape, 2)
    return jnp.where(row == padded - 1, lens[:, None, None, None], both)


def across(value, mask):
    return lax.ppermute(value, "rep", [(i, i ^ mask) for i in range(lax.axis_size("rep"))])


def along(value, pairs):
    return lax.ppermute(value, "tp", pairs)


def after(value, *earlier):
    return lax.optimization_barrier((value, *earlier))[0]


def pair_slots(group, blocks):
    match = blocks[:, None] == group[None, :]
    order = jnp.arange(group.shape[0], dtype=jnp.int32)[None, :]
    lowest = jnp.min(jnp.where(match, order, group.shape[0]), axis=1)
    highest = jnp.max(jnp.where(match, order, -1), axis=1)
    used = highest >= 0
    return [jnp.where(used, lowest, 0), jnp.where(used, highest, 0), used.astype(jnp.int32)]


def pair_bias(tree_mask):
    bias = jnp.where(tree_mask == 1, 0.0, NEG_FILL).astype(jnp.float32)
    tree = bias.shape[1]
    return jnp.pad(bias, ((0, 0), (0, 0), (0, -(-4 * tree // HD) * HD - tree)))


def local(
    queries,
    tree_cache,
    tree_mask,
    dest_group,
    accepted_path,
    prompt_cache,
    first_len,
    spill_cache,
    spill_len,
    out_weight,
    *,
    tuned,
):
    req, tree, cols = queries.shape
    prompt = prompt_cache.shape[2]
    padded = (prompt // 16 + 1) * 16
    group = dest_group[:, 0]

    if not tuned:
        accepted_cache = jnp.take_along_axis(tree_cache, accepted_path[:, None, :, None], axis=2)
        lens = jnp.stack([first_len[0], spill_len[0]]).astype(jnp.bfloat16)
        idx = jnp.stack([group, jnp.bitwise_xor(group, 1)])
        bias = jnp.where(tree_mask == 1, 0.0, NEG_FILL).astype(jnp.float32)
        bias = jnp.pad(bias, ((0, 0), (0, 0), (2 * padded, 0)))
        block = cache_block(prompt_cache, spill_cache, lens, 0, cols, padded)
        caches = lax.all_gather(block, "rep", axis=0, tiled=False)
        attn = attend(idx, queries, tree_cache, bias, [caches], 0, cols).reshape(req * tree, cols)
        whole = lax.all_gather(attn, "tp", axis=1, tiled=True)
        summed = jnp.dot(whole, out_weight, preferred_element_type=jnp.float32)
        return summed.astype(jnp.bfloat16).reshape(req, tree, out_weight.shape[1]), accepted_cache

    spill = across(spill_cache, 1)
    lens = jnp.stack([first_len[0], across(spill_len, 1)[0]]).astype(jnp.bfloat16)
    chunks = []
    start = 0
    for heads in HEAD_CHUNKS:
        chunks.append((start, heads * HD))
        start += heads * HD
    n = len(chunks)
    gathered, owns, raws = [], [], []

    def gather(i):
        start, width = chunks[i]
        block = cache_block(prompt_cache, spill, lens, start, width, padded)
        if i > 0:
            block = after(block, *gathered[i - 1][1:], *raws[max(i - 2, 0) : i - 1])
        gathered.append([block] + [across(block, m) for m in (2, 4, 6)])

    gather(0)
    queries, tree_cache = lax.optimization_barrier((queries, tree_cache, gathered[0][0]))[:2]
    other_queries = across(queries, 1)
    other_tree = across(tree_cache, 1)
    tree_mask, dest_group = lax.optimization_barrier((tree_mask, dest_group, gathered[0][FRONT]))[:2]
    other_mask = across(tree_mask, 1)
    group, other_group = dest_group[:, 0], across(dest_group, 1)[:, 0]
    me = lax.axis_index("rep").astype(jnp.int32)
    blocks = jnp.bitwise_xor(me, jnp.array([0, 2, 4, 6], jnp.int32))
    slots = jnp.stack(pair_slots(group, blocks) + pair_slots(other_group, blocks))
    sides = [queries, tree_cache, pair_bias(tree_mask), other_queries, other_tree, pair_bias(other_mask)]
    mine = jnp.bitwise_and(jnp.bitwise_xor(group, me), 1) == 0

    z = lax.axis_index("tp").astype(jnp.int32).reshape(1)
    weight = out_weight.reshape(lax.axis_size("tp"), cols, out_weight.shape[1])
    acc = None
    steps, outer, between = [], [], []
    for i in range(n + 2):
        fresh = []
        if i < n:
            start, width = chunks[i]
            ready = slots
            if i > 0:
                gates = [owns[i - 1]] + between[max(i - 2, 0) : i - 1]
                ready = after(slots, *gates)
            own, theirs = attend_pairs(ready, sides, gathered[i], start, 0, width)
            raws.append(theirs)
            if i + 1 < n:
                gather(i + 1)
                if GATE[0] == 1 or i > 0 and GATE[0] == 2:
                    theirs = after(theirs, *gathered[i + 1][1:])
            if i > 0 and GATE[1]:
                theirs = after(theirs, between[i - 1])
            if i > 0 and (GATE[2] == 1 or i < n - 1 and GATE[2] == 2 or i == 1 and GATE[2] == 3):
                theirs = after(theirs, outer[i - 1])
            attn = jnp.where(mine[:, None, None], own, across(theirs, 1)).reshape(req * tree, width)
            owns.append(attn)
            fresh = [attn]
        payload = fresh + ([between[i - 1]] if i > 0 else [])
        payload = jnp.concatenate(payload, axis=1)
        outer.append(along(payload, [(0, 1), (1, 0), (2, 3), (3, 2)] if i < n else [(1, 0), (2, 3)]))
        if i <= n:
            relayed = [outer[i - 1][:, : chunks[i - 1][1]]] if i > 0 else []
            between.append(along(jnp.concatenate(fresh + relayed, axis=1), [(1, 2), (2, 1)]))
        parts = [(0, *chunks[i]), (1, *chunks[i])] if i < n else []
        parts += [(2, *chunks[i - 1])] if 0 < i <= n else []
        parts += [(3, *chunks[i - 2])] if i > 1 else []
        steps.append(
            (owns[i] if i < n else None, outer[i], between[i - 1] if i > 0 else None, parts)
        )
        if i in SPLITS:
            acc = project(after(z, raws[-1]), weight, steps, acc, i == n + 1)
            steps = []
    path = after(accepted_path, owns[-1])
    accepted_cache = jnp.take_along_axis(tree_cache, path[:, None, :, None], axis=2)
    return acc.reshape(req, tree, out_weight.shape[1]), accepted_cache


def solution(mesh):
    heads_here = 32 // mesh.shape["tp"]
    tuned = mesh.shape["rep"] == 8 and mesh.shape["tp"] == 4 and heads_here == sum(HEAD_CHUNKS)
    return jax.shard_map(
        partial(local, tuned=tuned),
        mesh=mesh,
        in_specs=(
            P("rep", None, "tp"),
            P("rep", None, None, "tp"),
            P("rep", None, None),
            P("rep", None),
            P("rep", None),
            P("rep", None, None, "tp"),
            P("rep"),
            P("rep", None, None, "tp"),
            P("rep"),
            P(None, "tp"),
        ),
        out_specs=(P("rep", None, "tp"), P("rep", None, None, "tp")),
        check_vma=False,
    )
```

```python
import math
from functools import partial

import jax
import jax.numpy as jnp
from jax import lax
from jax.experimental import pallas as pl
from jax.experimental.pallas import tpu as pltpu
from jax.sharding import PartitionSpec as P

HD = 128
NEG_FILL = -1e30
HEAD_CHUNKS = (2, 2, 2, 2)
SPLITS = (2, 3, 4, 5)
FRONT = 1


K_FLOPS = 2_700_000_000
J_FLOPS = 2_000_000_000


def cost(flops):
    return pl.CostEstimate(flops=flops, bytes_accessed=1000, transcendentals=0)


SCALE = 1.0 / math.sqrt(HD)
LOG2E = math.log2(math.e)
VMEM_BYTES = 10 * 1024 * 1024
J_VMEM = 12 * 1024 * 1024


def attend_kernel(idx_ref, q_ref, tree_ref, bias_ref, *rest, n_caches):
    cache_refs = rest[:n_caches]
    out_ref, held, sems = rest[n_caches:]
    copies = []
    at = 0
    for i, ref in enumerate(cache_refs):
        size = ref.shape[0]
        copies.append(pltpu.make_async_copy(ref, held.at[pl.ds(at, size)], sems.at[i]))
        at += size
    for copy in copies:
        copy.start()
    for copy in copies:
        copy.wait()
    requests, _, width = q_ref.shape
    padded = held.shape[3]
    n_keys = bias_ref.shape[2]
    position = lax.broadcasted_iota(jnp.int32, (1, n_keys), 1).astype(jnp.float32)
    repeats = -(-n_keys // HD)

    def length_row(block, part):
        tail = held[block, part, 0, pl.ds(padded - 16, 16), 0:HD].astype(jnp.float32)[15:16]
        return jnp.concatenate([tail] * repeats, axis=1)[:, :n_keys]

    def body(r, carry):
        first = idx_ref[0, r]
        second = idx_ref[1, r]
        limit = jnp.where(position < padded, length_row(first, 0), length_row(second, 1) + padded)
        limit = jnp.where(position < 2 * padded, limit, n_keys)
        bias = bias_ref[r] + jnp.where(position < limit, 0.0, NEG_FILL)
        for h in range(width // HD):
            cols = slice(h * HD, (h + 1) * HD)
            keys = jnp.concatenate(
                [held[first, 0, 0, :, cols], held[second, 1, 0, :, cols], tree_ref[r, 0, :, cols]], axis=0
            )
            values = jnp.concatenate(
                [held[first, 0, 1, :, cols], held[second, 1, 1, :, cols], tree_ref[r, 1, :, cols]], axis=0
            )
            scores = lax.dot_general(
                q_ref[r, :, cols], keys, (((1,), (1,)), ((), ())), preferred_element_type=jnp.float32
            )
            scores = scores * SCALE + bias
            raw = jnp.exp(scores - jnp.max(scores, axis=1, keepdims=True))
            total = jnp.sum(raw, axis=1, keepdims=True)
            accum = jnp.dot(raw.astype(jnp.bfloat16), values, preferred_element_type=jnp.float32)
            out_ref[r, :, cols] = (accum / total).astype(out_ref.dtype)
        return carry

    lax.fori_loop(0, requests, body, 0)


def attend(idx, queries, tree_cache, bias, caches, start, width):
    req, tree, _ = queries.shape
    block = start // width
    n_blocks = sum(c.shape[0] for c in caches)
    keys = bias.shape[2]
    return pl.pallas_call(
        partial(attend_kernel, n_caches=len(caches)),
        grid=(1,),
        in_specs=[
            pl.BlockSpec(memory_space=pltpu.SMEM),
            pl.BlockSpec((req, tree, width), lambda i: (0, 0, block)),
            pl.BlockSpec((req, 2, tree, width), lambda i: (0, 0, 0, block)),
            pl.BlockSpec(bias.shape, lambda i: (0, 0, 0)),
        ]
        + [pl.BlockSpec(memory_space=pl.ANY)] * len(caches),
        out_specs=pl.BlockSpec((req, tree, width), lambda i: (0, 0, 0)),
        out_shape=jax.ShapeDtypeStruct((req, tree, width), jnp.bfloat16),
        scratch_shapes=[
            pltpu.VMEM((n_blocks,) + caches[0].shape[1:], jnp.bfloat16),
            pltpu.SemaphoreType.DMA((len(caches),)),
        ],
        compiler_params=pltpu.CompilerParams(vmem_limit_bytes=8 * VMEM_BYTES),
        cost_estimate=pl.CostEstimate(
            flops=4 * req * tree * keys * width * 16, bytes_accessed=8 * n_blocks * 320 * width, transcendentals=0
        ),
    )(idx, queries, tree_cache, bias, *caches)


def paired_kernel(slot_ref, *rest, start, inside, n_caches):
    sides, caches, outs = rest[:6], rest[6 : 6 + n_caches], rest[6 + n_caches :]
    width = outs[0].shape[2]
    tree = outs[0].shape[1]
    padded = caches[0].shape[2]
    own_keys = 4 * tree
    n_keys = own_keys + 2 * padded
    spill_at = own_keys + padded
    lanes = sides[2].shape[2]
    position = lax.broadcasted_iota(jnp.int32, (1, n_keys), 1).astype(jnp.float32)
    lane = lax.broadcasted_iota(jnp.int32, (tree, lanes), 1)
    repeats = -(-n_keys // HD)

    def length_row(ref, part):
        tail = ref[part, 0, padded - 16 : padded, 0:HD].astype(jnp.float32)[15:16]
        return jnp.concatenate([tail] * repeats, axis=1)[:, :n_keys]

    for m, cache in enumerate(caches):
        limit = jnp.where(position < spill_at, length_row(cache, 0) + own_keys, length_row(cache, 1) + spill_at)
        limit = jnp.where(position < own_keys, n_keys, limit)
        unseen = jnp.where(position < limit, 0.0, NEG_FILL)
        rows, used = [], []
        for side in range(2):
            for k in range(2):
                rows.append((side, slot_ref[3 * side + k, m]))
                used.append(slot_ref[3 * side + 2, m] > 0)
        head_bias = []
        for i, (side, r) in enumerate(rows):
            block = sides[3 * side + 2][r]
            block = block if i == 0 else pltpu.roll(block, i * tree, 1)
            here = jnp.logical_and(lane >= i * tree, lane < (i + 1) * tree)
            head_bias.append(jnp.where(here, block, jnp.where(lane < own_keys, NEG_FILL, 0.0)))
        bias = jnp.concatenate(
            [
                jnp.concatenate(head_bias, axis=0) + unseen[:, :lanes],
                jnp.broadcast_to(unseen[:, lanes:], (own_keys, n_keys - lanes)),
            ],
            axis=1,
        )
        results = []
        for h in range(width // HD):
            here = slice(h * HD, (h + 1) * HD)
            held = slice(inside + h * HD, inside + (h + 1) * HD)
            cols = slice(start + h * HD, start + (h + 1) * HD)

            def stored(k):
                own = [sides[3 * side + 1][r, k, :, cols] for side, r in rows]
                return jnp.concatenate(own + [cache[0, k, :, held], cache[1, k, :, held]], axis=0)

            asked = jnp.concatenate([sides[3 * side][r, :, cols] for side, r in rows], axis=0)
            scores = lax.dot_general(
                asked, stored(0), (((1,), (1,)), ((), ())), preferred_element_type=jnp.float32
            )
            scores = scores * (SCALE * LOG2E) + bias
            raw = jnp.exp2(scores - jnp.max(scores, axis=1, keepdims=True))
            total = jnp.sum(raw, axis=1, keepdims=True)
            accum = jnp.dot(raw.astype(jnp.bfloat16), stored(1), preferred_element_type=jnp.float32)
            results.append((here, (accum / total).astype(jnp.bfloat16)))
        for here, attn in results:
            for i, (side, r) in enumerate(rows):
                mine = attn[i * tree : (i + 1) * tree]
                outs[side][r, :, here] = jnp.where(used[i], mine, outs[side][r, :, here])


def attend_pairs(slots, sides, caches, start, inside, width):
    req, tree, _ = sides[0].shape
    vmem = pl.BlockSpec(memory_space=pltpu.VMEM)
    return pl.pallas_call(
        partial(paired_kernel, start=start, inside=inside, n_caches=len(caches)),
        in_specs=[pl.BlockSpec(memory_space=pltpu.SMEM)] + [vmem] * (len(sides) + len(caches)),
        out_specs=[vmem, vmem],
        out_shape=[jax.ShapeDtypeStruct((req, tree, width), jnp.bfloat16)] * 2,
        compiler_params=pltpu.CompilerParams(vmem_limit_bytes=VMEM_BYTES),
        cost_estimate=cost(K_FLOPS + K_FLOPS * width // HD),
    )(slots, *sides, *caches)


def project_kernel(z_ref, w_hbm, *rest, steps, has_acc):
    rest = list(rest)
    acc = rest.pop(0) if has_acc else None
    out_ref, w_ref, sems = rest[-3:]
    z = z_ref[0]
    lower = z < 2
    middle = jnp.logical_and(z > 0, z < 3)
    sources = (z, jnp.bitwise_xor(z, 1), jnp.where(lower, 2, 1), jnp.where(lower, 3, 0))
    copies = []
    at = 0
    for _, _, step in steps:
        for which, start, width in step:
            copies.append(
                pltpu.make_async_copy(
                    w_hbm.at[sources[which], pl.ds(start, width), :],
                    w_ref.at[pl.ds(at, width), :],
                    sems.at[len(copies)],
                )
            )
            copies[-1].start()
            at += width
    pieces = []
    for has_own, has_middle, _ in steps:
        own = rest.pop(0) if has_own else None
        outer = rest.pop(0)
        fresh = own.shape[1] if has_own else 0
        if has_own:
            pieces += [own[...], outer[:, :fresh]]
        if has_middle:
            pieces.append(jnp.where(middle, rest.pop(0)[...], outer[:, fresh:]))
    attn = jnp.concatenate(pieces, axis=1)
    for copy in copies:
        copy.wait()
    tile = 256
    for n in range(out_ref.shape[1] // tile):
        cols = slice(n * tile, (n + 1) * tile)
        total = jnp.dot(attn, w_ref[:, cols], preferred_element_type=jnp.float32)
        if has_acc:
            total += acc[:, cols]
        out_ref[:, cols] = total.astype(out_ref.dtype)


def project(z, weight, steps, acc, last):
    _, _, cols = weight.shape
    given = [] if acc is None else [acc]
    shape = []
    for own, outer, between, parts in steps:
        given += [v for v in (own, outer, between) if v is not None]
        shape.append((own is not None, between is not None, tuple(parts)))
    count = sum(len(step[2]) for step in shape)
    depth = sum(width for step in shape for _, _, width in step[2])
    rows = steps[0][1].shape[0]
    vmem = pl.BlockSpec(memory_space=pltpu.VMEM)
    return pl.pallas_call(
        partial(project_kernel, steps=tuple(shape), has_acc=acc is not None),
        in_specs=[pl.BlockSpec(memory_space=pltpu.SMEM), pl.BlockSpec(memory_space=pltpu.HBM)] + [vmem] * len(given),
        out_specs=vmem,
        out_shape=jax.ShapeDtypeStruct((rows, cols), jnp.bfloat16 if last else jnp.float32),
        scratch_shapes=[
            pltpu.VMEM((depth, cols), jnp.bfloat16),
            pltpu.SemaphoreType.DMA((count,)),
        ],
        input_output_aliases={2: 0} if acc is not None and not last else {},
        compiler_params=pltpu.CompilerParams(vmem_limit_bytes=J_VMEM),
        cost_estimate=cost(J_FLOPS),
    )(z, weight, *given)


def cache_block(prompt, spill, lens, start, width, padded):
    both = jnp.stack([prompt[0, ..., start : start + width], spill[0, ..., start : start + width]])
    both = jnp.pad(both, ((0, 0), (0, 0), (0, padded - both.shape[2]), (0, 0)))
    row = lax.broadcasted_iota(jnp.int32, both.shape, 2)
    return jnp.where(row == padded - 1, lens[:, None, None, None], both)


def across(value, mask):
    return lax.ppermute(value, "rep", [(i, i ^ mask) for i in range(lax.axis_size("rep"))])


def along(value, pairs):
    return lax.ppermute(value, "tp", pairs)


def after(value, *earlier):
    return lax.optimization_barrier((value, *earlier))[0]


def pair_slots(group, blocks):
    match = blocks[:, None] == group[None, :]
    order = jnp.arange(group.shape[0], dtype=jnp.int32)[None, :]
    lowest = jnp.min(jnp.where(match, order, group.shape[0]), axis=1)
    highest = jnp.max(jnp.where(match, order, -1), axis=1)
    used = highest >= 0
    return [jnp.where(used, lowest, 0), jnp.where(used, highest, 0), used.astype(jnp.int32)]


def pair_bias(tree_mask):
    bias = jnp.where(tree_mask == 1, 0.0, NEG_FILL).astype(jnp.float32)
    tree = bias.shape[1]
    return jnp.pad(bias, ((0, 0), (0, 0), (0, -(-4 * tree // HD) * HD - tree)))


def local(
    queries,
    tree_cache,
    tree_mask,
    dest_group,
    accepted_path,
    prompt_cache,
    first_len,
    spill_cache,
    spill_len,
    out_weight,
    *,
    tuned,
):
    req, tree, cols = queries.shape
    prompt = prompt_cache.shape[2]
    padded = (prompt // 16 + 1) * 16
    group = dest_group[:, 0]

    if not tuned:
        accepted_cache = jnp.take_along_axis(tree_cache, accepted_path[:, None, :, None], axis=2)
        lens = jnp.stack([first_len[0], spill_len[0]]).astype(jnp.bfloat16)
        idx = jnp.stack([group, jnp.bitwise_xor(group, 1)])
        bias = jnp.where(tree_mask == 1, 0.0, NEG_FILL).astype(jnp.float32)
        bias = jnp.pad(bias, ((0, 0), (0, 0), (2 * padded, 0)))
        block = cache_block(prompt_cache, spill_cache, lens, 0, cols, padded)
        caches = lax.all_gather(block, "rep", axis=0, tiled=False)
        attn = attend(idx, queries, tree_cache, bias, [caches], 0, cols).reshape(req * tree, cols)
        whole = lax.all_gather(attn, "tp", axis=1, tiled=True)
        summed = jnp.dot(whole, out_weight, preferred_element_type=jnp.float32)
        return summed.astype(jnp.bfloat16).reshape(req, tree, out_weight.shape[1]), accepted_cache

    spill = across(spill_cache, 1)
    lens = jnp.stack([first_len[0], across(spill_len, 1)[0]]).astype(jnp.bfloat16)
    chunks = []
    start = 0
    for heads in HEAD_CHUNKS:
        chunks.append((start, heads * HD))
        start += heads * HD
    n = len(chunks)
    gathered, owns, raws = [], [], []

    def gather(i):
        start, width = chunks[i]
        block = cache_block(prompt_cache, spill, lens, start, width, padded)
        if i > 0:
            block = after(block, *gathered[i - 1][1:], *raws[max(i - 2, 0) : i - 1])
        gathered.append([block] + [across(block, m) for m in (2, 4, 6)])

    gather(0)
    queries, tree_cache = lax.optimization_barrier((queries, tree_cache, gathered[0][0]))[:2]
    other_queries = across(queries, 1)
    other_tree = across(tree_cache, 1)
    tree_mask, dest_group = lax.optimization_barrier((tree_mask, dest_group, gathered[0][FRONT]))[:2]
    other_mask = across(tree_mask, 1)
    group, other_group = dest_group[:, 0], across(dest_group, 1)[:, 0]
    me = lax.axis_index("rep").astype(jnp.int32)
    blocks = jnp.bitwise_xor(me, jnp.array([0, 2, 4, 6], jnp.int32))
    slots = jnp.stack(pair_slots(group, blocks) + pair_slots(other_group, blocks))
    sides = [queries, tree_cache, pair_bias(tree_mask), other_queries, other_tree, pair_bias(other_mask)]
    mine = jnp.bitwise_and(jnp.bitwise_xor(group, me), 1) == 0

    z = lax.axis_index("tp").astype(jnp.int32).reshape(1)
    weight = out_weight.reshape(lax.axis_size("tp"), cols, out_weight.shape[1])
    acc = None
    steps, outer, between = [], [], []
    for i in range(n + 2):
        fresh = []
        if i < n:
            start, width = chunks[i]
            ready = slots
            if i > 0:
                gates = [owns[i - 1]] + between[max(i - 2, 0) : i - 1]
                ready = after(slots, *gates)
            own, theirs = attend_pairs(ready, sides, gathered[i], start, 0, width)
            raws.append(theirs)
            if i + 1 < n:
                gather(i + 1)
            if i > 0:
                theirs = after(theirs, between[i - 1])
            if 0 < i < n - 1:
                theirs = after(theirs, outer[i - 1])
            attn = jnp.where(mine[:, None, None], own, across(theirs, 1)).reshape(req * tree, width)
            owns.append(attn)
            fresh = [attn]
        payload = fresh + ([between[i - 1]] if i > 0 else [])
        payload = jnp.concatenate(payload, axis=1)
        outer.append(along(payload, [(0, 1), (1, 0), (2, 3), (3, 2)] if i < n else [(1, 0), (2, 3)]))
        if i <= n:
            relayed = [outer[i - 1][:, : chunks[i - 1][1]]] if i > 0 else []
            between.append(along(jnp.concatenate(fresh + relayed, axis=1), [(1, 2), (2, 1)]))
        parts = [(0, *chunks[i]), (1, *chunks[i])] if i < n else []
        parts += [(2, *chunks[i - 1])] if 0 < i <= n else []
        parts += [(3, *chunks[i - 2])] if i > 1 else []
        steps.append(
            (owns[i] if i < n else None, outer[i], between[i - 1] if i > 0 else None, parts)
        )
        if i in SPLITS:
            acc = project(after(z, raws[-1]), weight, steps, acc, i == n + 1)
            steps = []
    path = after(accepted_path, outer[n - 1])
    accepted_cache = jnp.take_along_axis(tree_cache, path[:, None, :, None], axis=2)
    return acc.reshape(req, tree, out_weight.shape[1]), accepted_cache


def solution(mesh):
    heads_here = 32 // mesh.shape["tp"]
    tuned = mesh.shape["rep"] == 8 and mesh.shape["tp"] == 4 and heads_here == sum(HEAD_CHUNKS)
    return jax.shard_map(
        partial(local, tuned=tuned),
        mesh=mesh,
        in_specs=(
            P("rep", None, "tp"),
            P("rep", None, None, "tp"),
            P("rep", None, None),
            P("rep", None),
            P("rep", None),
            P("rep", None, None, "tp"),
            P("rep"),
            P("rep", None, None, "tp"),
            P("rep"),
            P(None, "tp"),
        ),
        out_specs=(P("rep", None, "tp"), P("rep", None, None, "tp")),
        check_vma=False,
    )
```

```python
import math
from functools import partial

import jax
import jax.numpy as jnp
from jax import lax
from jax.experimental import pallas as pl
from jax.experimental.pallas import tpu as pltpu
from jax.sharding import PartitionSpec as P

HD = 128
NEG_FILL = -1e30
HEAD_CHUNKS = (2, 2, 2, 2)
SPLITS = (2, 3, 4, 5)
FRONT = 1


K_FLOPS = 2_700_000_000
J_FLOPS = 2_000_000_000


def cost(flops):
    return pl.CostEstimate(flops=flops, bytes_accessed=1000, transcendentals=0)


SCALE = 1.0 / math.sqrt(HD)
LOG2E = math.log2(math.e)
VMEM_BYTES = 10 * 1024 * 1024
J_VMEM = 12 * 1024 * 1024


def attend_kernel(idx_ref, q_ref, tree_ref, bias_ref, *rest, n_caches):
    cache_refs = rest[:n_caches]
    out_ref, held, sems = rest[n_caches:]
    copies = []
    at = 0
    for i, ref in enumerate(cache_refs):
        size = ref.shape[0]
        copies.append(pltpu.make_async_copy(ref, held.at[pl.ds(at, size)], sems.at[i]))
        at += size
    for copy in copies:
        copy.start()
    for copy in copies:
        copy.wait()
    requests, _, width = q_ref.shape
    padded = held.shape[3]
    n_keys = bias_ref.shape[2]
    position = lax.broadcasted_iota(jnp.int32, (1, n_keys), 1).astype(jnp.float32)
    repeats = -(-n_keys // HD)

    def length_row(block, part):
        tail = held[block, part, 0, pl.ds(padded - 16, 16), 0:HD].astype(jnp.float32)[15:16]
        return jnp.concatenate([tail] * repeats, axis=1)[:, :n_keys]

    def body(r, carry):
        first = idx_ref[0, r]
        second = idx_ref[1, r]
        limit = jnp.where(position < padded, length_row(first, 0), length_row(second, 1) + padded)
        limit = jnp.where(position < 2 * padded, limit, n_keys)
        bias = bias_ref[r] + jnp.where(position < limit, 0.0, NEG_FILL)
        for h in range(width // HD):
            cols = slice(h * HD, (h + 1) * HD)
            keys = jnp.concatenate(
                [held[first, 0, 0, :, cols], held[second, 1, 0, :, cols], tree_ref[r, 0, :, cols]], axis=0
            )
            values = jnp.concatenate(
                [held[first, 0, 1, :, cols], held[second, 1, 1, :, cols], tree_ref[r, 1, :, cols]], axis=0
            )
            scores = lax.dot_general(
                q_ref[r, :, cols], keys, (((1,), (1,)), ((), ())), preferred_element_type=jnp.float32
            )
            scores = scores * SCALE + bias
            raw = jnp.exp(scores - jnp.max(scores, axis=1, keepdims=True))
            total = jnp.sum(raw, axis=1, keepdims=True)
            accum = jnp.dot(raw.astype(jnp.bfloat16), values, preferred_element_type=jnp.float32)
            out_ref[r, :, cols] = (accum / total).astype(out_ref.dtype)
        return carry

    lax.fori_loop(0, requests, body, 0)


def attend(idx, queries, tree_cache, bias, caches, start, width):
    req, tree, _ = queries.shape
    block = start // width
    n_blocks = sum(c.shape[0] for c in caches)
    keys = bias.shape[2]
    return pl.pallas_call(
        partial(attend_kernel, n_caches=len(caches)),
        grid=(1,),
        in_specs=[
            pl.BlockSpec(memory_space=pltpu.SMEM),
            pl.BlockSpec((req, tree, width), lambda i: (0, 0, block)),
            pl.BlockSpec((req, 2, tree, width), lambda i: (0, 0, 0, block)),
            pl.BlockSpec(bias.shape, lambda i: (0, 0, 0)),
        ]
        + [pl.BlockSpec(memory_space=pl.ANY)] * len(caches),
        out_specs=pl.BlockSpec((req, tree, width), lambda i: (0, 0, 0)),
        out_shape=jax.ShapeDtypeStruct((req, tree, width), jnp.bfloat16),
        scratch_shapes=[
            pltpu.VMEM((n_blocks,) + caches[0].shape[1:], jnp.bfloat16),
            pltpu.SemaphoreType.DMA((len(caches),)),
        ],
        compiler_params=pltpu.CompilerParams(vmem_limit_bytes=8 * VMEM_BYTES),
        cost_estimate=pl.CostEstimate(
            flops=4 * req * tree * keys * width * 16, bytes_accessed=8 * n_blocks * 320 * width, transcendentals=0
        ),
    )(idx, queries, tree_cache, bias, *caches)


def paired_kernel(slot_ref, *rest, start, inside, n_caches):
    sides, caches, outs = rest[:6], rest[6 : 6 + n_caches], rest[6 + n_caches :]
    width = outs[0].shape[2]
    tree = outs[0].shape[1]
    padded = caches[0].shape[2]
    own_keys = 4 * tree
    n_keys = own_keys + 2 * padded
    spill_at = own_keys + padded
    lanes = sides[2].shape[2]
    position = lax.broadcasted_iota(jnp.int32, (1, n_keys), 1).astype(jnp.float32)
    lane = lax.broadcasted_iota(jnp.int32, (tree, lanes), 1)
    repeats = -(-n_keys // HD)

    def length_row(ref, part):
        tail = ref[part, 0, padded - 16 : padded, 0:HD].astype(jnp.float32)[15:16]
        return jnp.concatenate([tail] * repeats, axis=1)[:, :n_keys]

    for m, cache in enumerate(caches):
        limit = jnp.where(position < spill_at, length_row(cache, 0) + own_keys, length_row(cache, 1) + spill_at)
        limit = jnp.where(position < own_keys, n_keys, limit)
        unseen = jnp.where(position < limit, 0.0, NEG_FILL)
        rows, used = [], []
        for side in range(2):
            for k in range(2):
                rows.append((side, slot_ref[3 * side + k, m]))
                used.append(slot_ref[3 * side + 2, m] > 0)
        head_bias = []
        for i, (side, r) in enumerate(rows):
            block = sides[3 * side + 2][r]
            block = block if i == 0 else pltpu.roll(block, i * tree, 1)
            here = jnp.logical_and(lane >= i * tree, lane < (i + 1) * tree)
            head_bias.append(jnp.where(here, block, jnp.where(lane < own_keys, NEG_FILL, 0.0)))
        bias = jnp.concatenate(
            [
                jnp.concatenate(head_bias, axis=0) + unseen[:, :lanes],
                jnp.broadcast_to(unseen[:, lanes:], (own_keys, n_keys - lanes)),
            ],
            axis=1,
        )
        results = []
        for h in range(width // HD):
            here = slice(h * HD, (h + 1) * HD)
            held = slice(inside + h * HD, inside + (h + 1) * HD)
            cols = slice(start + h * HD, start + (h + 1) * HD)

            def stored(k):
                own = [sides[3 * side + 1][r, k, :, cols] for side, r in rows]
                return jnp.concatenate(own + [cache[0, k, :, held], cache[1, k, :, held]], axis=0)

            asked = jnp.concatenate([sides[3 * side][r, :, cols] for side, r in rows], axis=0)
            scores = lax.dot_general(
                asked, stored(0), (((1,), (1,)), ((), ())), preferred_element_type=jnp.float32
            )
            scores = scores * (SCALE * LOG2E) + bias
            raw = jnp.exp2(scores - jnp.max(scores, axis=1, keepdims=True))
            total = jnp.sum(raw, axis=1, keepdims=True)
            accum = jnp.dot(raw.astype(jnp.bfloat16), stored(1), preferred_element_type=jnp.float32)
            results.append((here, (accum / total).astype(jnp.bfloat16)))
        for here, attn in results:
            for i, (side, r) in enumerate(rows):
                mine = attn[i * tree : (i + 1) * tree]
                outs[side][r, :, here] = jnp.where(used[i], mine, outs[side][r, :, here])


def attend_pairs(slots, sides, caches, start, inside, width):
    req, tree, _ = sides[0].shape
    vmem = pl.BlockSpec(memory_space=pltpu.VMEM)
    return pl.pallas_call(
        partial(paired_kernel, start=start, inside=inside, n_caches=len(caches)),
        in_specs=[pl.BlockSpec(memory_space=pltpu.SMEM)] + [vmem] * (len(sides) + len(caches)),
        out_specs=[vmem, vmem],
        out_shape=[jax.ShapeDtypeStruct((req, tree, width), jnp.bfloat16)] * 2,
        compiler_params=pltpu.CompilerParams(vmem_limit_bytes=VMEM_BYTES),
        cost_estimate=cost(K_FLOPS + K_FLOPS * width // HD),
    )(slots, *sides, *caches)


def project_kernel(z_ref, w_hbm, *rest, steps, has_acc):
    rest = list(rest)
    acc = rest.pop(0) if has_acc else None
    out_ref, w_ref, sems = rest[-3:]
    z = z_ref[0]
    lower = z < 2
    middle = jnp.logical_and(z > 0, z < 3)
    sources = (z, jnp.bitwise_xor(z, 1), jnp.where(lower, 2, 1), jnp.where(lower, 3, 0))
    copies = []
    at = 0
    for _, _, step in steps:
        for which, start, width in step:
            copies.append(
                pltpu.make_async_copy(
                    w_hbm.at[sources[which], pl.ds(start, width), :],
                    w_ref.at[pl.ds(at, width), :],
                    sems.at[len(copies)],
                )
            )
            copies[-1].start()
            at += width
    pieces = []
    for has_own, has_middle, _ in steps:
        own = rest.pop(0) if has_own else None
        outer = rest.pop(0)
        fresh = own.shape[1] if has_own else 0
        if has_own:
            pieces += [own[...], outer[:, :fresh]]
        if has_middle:
            pieces.append(jnp.where(middle, rest.pop(0)[...], outer[:, fresh:]))
    attn = jnp.concatenate(pieces, axis=1)
    for copy in copies:
        copy.wait()
    tile = 256
    for n in range(out_ref.shape[1] // tile):
        cols = slice(n * tile, (n + 1) * tile)
        total = jnp.dot(attn, w_ref[:, cols], preferred_element_type=jnp.float32)
        if has_acc:
            total += acc[:, cols]
        out_ref[:, cols] = total.astype(out_ref.dtype)


def project(z, weight, steps, acc, last):
    _, _, cols = weight.shape
    given = [] if acc is None else [acc]
    shape = []
    for own, outer, between, parts in steps:
        given += [v for v in (own, outer, between) if v is not None]
        shape.append((own is not None, between is not None, tuple(parts)))
    count = sum(len(step[2]) for step in shape)
    depth = sum(width for step in shape for _, _, width in step[2])
    rows = steps[0][1].shape[0]
    vmem = pl.BlockSpec(memory_space=pltpu.VMEM)
    return pl.pallas_call(
        partial(project_kernel, steps=tuple(shape), has_acc=acc is not None),
        in_specs=[pl.BlockSpec(memory_space=pltpu.SMEM), pl.BlockSpec(memory_space=pltpu.HBM)] + [vmem] * len(given),
        out_specs=vmem,
        out_shape=jax.ShapeDtypeStruct((rows, cols), jnp.bfloat16 if last else jnp.float32),
        scratch_shapes=[
            pltpu.VMEM((depth, cols), jnp.bfloat16),
            pltpu.SemaphoreType.DMA((count,)),
        ],
        input_output_aliases={2: 0} if acc is not None and not last else {},
        compiler_params=pltpu.CompilerParams(vmem_limit_bytes=J_VMEM),
        cost_estimate=cost(J_FLOPS),
    )(z, weight, *given)


def accept_kernel(pick_ref, tree_ref, out_ref):
    for r in range(tree_ref.shape[0]):
        for k in range(2):
            rows = jnp.dot(pick_ref[r], tree_ref[r, k], preferred_element_type=jnp.float32)
            out_ref[r, k] = rows[: out_ref.shape[2]].astype(out_ref.dtype)


def accept(path, tree_cache):
    req, _, tree, cols = tree_cache.shape
    taken = path.shape[1]
    order = jnp.arange(tree, dtype=jnp.int32)
    pick = (path[:, :, None] == order[None, None, :]).astype(jnp.bfloat16)
    pick = jnp.pad(pick, ((0, 0), (0, -taken % 16), (0, 0)))
    vmem = pl.BlockSpec(memory_space=pltpu.VMEM)
    return pl.pallas_call(
        accept_kernel,
        in_specs=[vmem, vmem],
        out_specs=vmem,
        out_shape=jax.ShapeDtypeStruct((req, 2, taken, cols), jnp.bfloat16),
        compiler_params=pltpu.CompilerParams(vmem_limit_bytes=VMEM_BYTES),
        cost_estimate=cost(J_FLOPS),
    )(pick, tree_cache)


def cache_block(prompt, spill, lens, start, width, padded):
    both = jnp.stack([prompt[0, ..., start : start + width], spill[0, ..., start : start + width]])
    both = jnp.pad(both, ((0, 0), (0, 0), (0, padded - both.shape[2]), (0, 0)))
    row = lax.broadcasted_iota(jnp.int32, both.shape, 2)
    return jnp.where(row == padded - 1, lens[:, None, None, None], both)


def across(value, mask):
    return lax.ppermute(value, "rep", [(i, i ^ mask) for i in range(lax.axis_size("rep"))])


def along(value, pairs):
    return lax.ppermute(value, "tp", pairs)


def after(value, *earlier):
    return lax.optimization_barrier((value, *earlier))[0]


def pair_slots(group, blocks):
    match = blocks[:, None] == group[None, :]
    order = jnp.arange(group.shape[0], dtype=jnp.int32)[None, :]
    lowest = jnp.min(jnp.where(match, order, group.shape[0]), axis=1)
    highest = jnp.max(jnp.where(match, order, -1), axis=1)
    used = highest >= 0
    return [jnp.where(used, lowest, 0), jnp.where(used, highest, 0), used.astype(jnp.int32)]


def pair_bias(tree_mask):
    bias = jnp.where(tree_mask == 1, 0.0, NEG_FILL).astype(jnp.float32)
    tree = bias.shape[1]
    return jnp.pad(bias, ((0, 0), (0, 0), (0, -(-4 * tree // HD) * HD - tree)))


def local(
    queries,
    tree_cache,
    tree_mask,
    dest_group,
    accepted_path,
    prompt_cache,
    first_len,
    spill_cache,
    spill_len,
    out_weight,
    *,
    tuned,
):
    req, tree, cols = queries.shape
    prompt = prompt_cache.shape[2]
    padded = (prompt // 16 + 1) * 16
    group = dest_group[:, 0]

    if not tuned:
        accepted_cache = jnp.take_along_axis(tree_cache, accepted_path[:, None, :, None], axis=2)
        lens = jnp.stack([first_len[0], spill_len[0]]).astype(jnp.bfloat16)
        idx = jnp.stack([group, jnp.bitwise_xor(group, 1)])
        bias = jnp.where(tree_mask == 1, 0.0, NEG_FILL).astype(jnp.float32)
        bias = jnp.pad(bias, ((0, 0), (0, 0), (2 * padded, 0)))
        block = cache_block(prompt_cache, spill_cache, lens, 0, cols, padded)
        caches = lax.all_gather(block, "rep", axis=0, tiled=False)
        attn = attend(idx, queries, tree_cache, bias, [caches], 0, cols).reshape(req * tree, cols)
        whole = lax.all_gather(attn, "tp", axis=1, tiled=True)
        summed = jnp.dot(whole, out_weight, preferred_element_type=jnp.float32)
        return summed.astype(jnp.bfloat16).reshape(req, tree, out_weight.shape[1]), accepted_cache

    spill = across(spill_cache, 1)
    lens = jnp.stack([first_len[0], across(spill_len, 1)[0]]).astype(jnp.bfloat16)
    chunks = []
    start = 0
    for heads in HEAD_CHUNKS:
        chunks.append((start, heads * HD))
        start += heads * HD
    n = len(chunks)
    gathered, owns, raws = [], [], []

    def gather(i):
        start, width = chunks[i]
        block = cache_block(prompt_cache, spill, lens, start, width, padded)
        if i > 0:
            block = after(block, *gathered[i - 1][1:])
        gathered.append([block] + [across(block, m) for m in (2, 4, 6)])

    gather(0)
    queries, tree_cache = lax.optimization_barrier((queries, tree_cache, gathered[0][0]))[:2]
    other_queries = across(queries, 1)
    other_tree = across(tree_cache, 1)
    tree_mask, dest_group = lax.optimization_barrier((tree_mask, dest_group, gathered[0][FRONT]))[:2]
    other_mask = across(tree_mask, 1)
    group, other_group = dest_group[:, 0], across(dest_group, 1)[:, 0]
    me = lax.axis_index("rep").astype(jnp.int32)
    blocks = jnp.bitwise_xor(me, jnp.array([0, 2, 4, 6], jnp.int32))
    slots = jnp.stack(pair_slots(group, blocks) + pair_slots(other_group, blocks))
    sides = [queries, tree_cache, pair_bias(tree_mask), other_queries, other_tree, pair_bias(other_mask)]
    mine = jnp.bitwise_and(jnp.bitwise_xor(group, me), 1) == 0

    z = lax.axis_index("tp").astype(jnp.int32).reshape(1)
    weight = out_weight.reshape(lax.axis_size("tp"), cols, out_weight.shape[1])
    acc = None
    steps, outer, between = [], [], []
    for i in range(n + 2):
        fresh = []
        if i < n:
            start, width = chunks[i]
            ready = slots
            if i > 0:
                gates = [owns[i - 1]] + between[max(i - 2, 0) : i - 1]
                ready = after(slots, *gates)
            own, theirs = attend_pairs(ready, sides, gathered[i], start, 0, width)
            raws.append(theirs)
            if i + 1 < n:
                gather(i + 1)
            if i > 0:
                theirs = after(theirs, between[i - 1])
            if 0 < i < n - 1:
                theirs = after(theirs, outer[i - 1])
            attn = jnp.where(mine[:, None, None], own, across(theirs, 1)).reshape(req * tree, width)
            owns.append(attn)
            fresh = [attn]
        payload = fresh + ([between[i - 1]] if i > 0 else [])
        payload = jnp.concatenate(payload, axis=1)
        outer.append(along(payload, [(0, 1), (1, 0), (2, 3), (3, 2)] if i < n else [(1, 0), (2, 3)]))
        if i <= n:
            relayed = [outer[i - 1][:, : chunks[i - 1][1]]] if i > 0 else []
            between.append(along(jnp.concatenate(fresh + relayed, axis=1), [(1, 2), (2, 1)]))
        parts = [(0, *chunks[i]), (1, *chunks[i])] if i < n else []
        parts += [(2, *chunks[i - 1])] if 0 < i <= n else []
        parts += [(3, *chunks[i - 2])] if i > 1 else []
        steps.append(
            (owns[i] if i < n else None, outer[i], between[i - 1] if i > 0 else None, parts)
        )
        if i in SPLITS:
            acc = project(after(z, raws[-1]), weight, steps, acc, i == n + 1)
            steps = []
    path = after(accepted_path, outer[n - 1])
    accepted_cache = accept(path, tree_cache)
    return acc.reshape(req, tree, out_weight.shape[1]), accepted_cache


def solution(mesh):
    heads_here = 32 // mesh.shape["tp"]
    tuned = mesh.shape["rep"] == 8 and mesh.shape["tp"] == 4 and heads_here == sum(HEAD_CHUNKS)
    return jax.shard_map(
        partial(local, tuned=tuned),
        mesh=mesh,
        in_specs=(
            P("rep", None, "tp"),
            P("rep", None, None, "tp"),
            P("rep", None, None),
            P("rep", None),
            P("rep", None),
            P("rep", None, None, "tp"),
            P("rep"),
            P("rep", None, None, "tp"),
            P("rep"),
            P(None, "tp"),
        ),
        out_specs=(P("rep", None, "tp"), P("rep", None, None, "tp")),
        check_vma=False,
    )
```

```python
import math
from functools import partial

import jax
import jax.numpy as jnp
from jax import lax
from jax.experimental import pallas as pl
from jax.experimental.pallas import tpu as pltpu
from jax.sharding import PartitionSpec as P

HD = 128
NEG_FILL = -1e30
HEAD_CHUNKS = (2, 2, 2, 2)
SPLITS = (2, 3, 5)
FRONT = 1


K_FLOPS = 2_700_000_000
J_FLOPS = 2_000_000_000


def cost(flops):
    return pl.CostEstimate(flops=flops, bytes_accessed=1000, transcendentals=0)


SCALE = 1.0 / math.sqrt(HD)
LOG2E = math.log2(math.e)
VMEM_BYTES = 10 * 1024 * 1024
J_VMEM = 12 * 1024 * 1024


def attend_kernel(idx_ref, q_ref, tree_ref, bias_ref, *rest, n_caches):
    cache_refs = rest[:n_caches]
    out_ref, held, sems = rest[n_caches:]
    copies = []
    at = 0
    for i, ref in enumerate(cache_refs):
        size = ref.shape[0]
        copies.append(pltpu.make_async_copy(ref, held.at[pl.ds(at, size)], sems.at[i]))
        at += size
    for copy in copies:
        copy.start()
    for copy in copies:
        copy.wait()
    requests, _, width = q_ref.shape
    padded = held.shape[3]
    n_keys = bias_ref.shape[2]
    position = lax.broadcasted_iota(jnp.int32, (1, n_keys), 1).astype(jnp.float32)
    repeats = -(-n_keys // HD)

    def length_row(block, part):
        tail = held[block, part, 0, pl.ds(padded - 16, 16), 0:HD].astype(jnp.float32)[15:16]
        return jnp.concatenate([tail] * repeats, axis=1)[:, :n_keys]

    def body(r, carry):
        first = idx_ref[0, r]
        second = idx_ref[1, r]
        limit = jnp.where(position < padded, length_row(first, 0), length_row(second, 1) + padded)
        limit = jnp.where(position < 2 * padded, limit, n_keys)
        bias = bias_ref[r] + jnp.where(position < limit, 0.0, NEG_FILL)
        for h in range(width // HD):
            cols = slice(h * HD, (h + 1) * HD)
            keys = jnp.concatenate(
                [held[first, 0, 0, :, cols], held[second, 1, 0, :, cols], tree_ref[r, 0, :, cols]], axis=0
            )
            values = jnp.concatenate(
                [held[first, 0, 1, :, cols], held[second, 1, 1, :, cols], tree_ref[r, 1, :, cols]], axis=0
            )
            scores = lax.dot_general(
                q_ref[r, :, cols], keys, (((1,), (1,)), ((), ())), preferred_element_type=jnp.float32
            )
            scores = scores * SCALE + bias
            raw = jnp.exp(scores - jnp.max(scores, axis=1, keepdims=True))
            total = jnp.sum(raw, axis=1, keepdims=True)
            accum = jnp.dot(raw.astype(jnp.bfloat16), values, preferred_element_type=jnp.float32)
            out_ref[r, :, cols] = (accum / total).astype(out_ref.dtype)
        return carry

    lax.fori_loop(0, requests, body, 0)


def attend(idx, queries, tree_cache, bias, caches, start, width):
    req, tree, _ = queries.shape
    block = start // width
    n_blocks = sum(c.shape[0] for c in caches)
    keys = bias.shape[2]
    return pl.pallas_call(
        partial(attend_kernel, n_caches=len(caches)),
        grid=(1,),
        in_specs=[
            pl.BlockSpec(memory_space=pltpu.SMEM),
            pl.BlockSpec((req, tree, width), lambda i: (0, 0, block)),
            pl.BlockSpec((req, 2, tree, width), lambda i: (0, 0, 0, block)),
            pl.BlockSpec(bias.shape, lambda i: (0, 0, 0)),
        ]
        + [pl.BlockSpec(memory_space=pl.ANY)] * len(caches),
        out_specs=pl.BlockSpec((req, tree, width), lambda i: (0, 0, 0)),
        out_shape=jax.ShapeDtypeStruct((req, tree, width), jnp.bfloat16),
        scratch_shapes=[
            pltpu.VMEM((n_blocks,) + caches[0].shape[1:], jnp.bfloat16),
            pltpu.SemaphoreType.DMA((len(caches),)),
        ],
        compiler_params=pltpu.CompilerParams(vmem_limit_bytes=8 * VMEM_BYTES),
        cost_estimate=pl.CostEstimate(
            flops=4 * req * tree * keys * width * 16, bytes_accessed=8 * n_blocks * 320 * width, transcendentals=0
        ),
    )(idx, queries, tree_cache, bias, *caches)


def paired_kernel(slot_ref, *rest, start, inside, n_caches):
    sides, caches, outs = rest[:6], rest[6 : 6 + n_caches], rest[6 + n_caches :]
    width = outs[0].shape[2]
    tree = outs[0].shape[1]
    padded = caches[0].shape[2]
    own_keys = 4 * tree
    n_keys = own_keys + 2 * padded
    spill_at = own_keys + padded
    lanes = sides[2].shape[2]
    position = lax.broadcasted_iota(jnp.int32, (1, n_keys), 1).astype(jnp.float32)
    lane = lax.broadcasted_iota(jnp.int32, (tree, lanes), 1)
    repeats = -(-n_keys // HD)

    def length_row(ref, part):
        tail = ref[part, 0, padded - 16 : padded, 0:HD].astype(jnp.float32)[15:16]
        return jnp.concatenate([tail] * repeats, axis=1)[:, :n_keys]

    for m, cache in enumerate(caches):
        limit = jnp.where(position < spill_at, length_row(cache, 0) + own_keys, length_row(cache, 1) + spill_at)
        limit = jnp.where(position < own_keys, n_keys, limit)
        unseen = jnp.where(position < limit, 0.0, NEG_FILL)
        rows, used = [], []
        for side in range(2):
            for k in range(2):
                rows.append((side, slot_ref[3 * side + k, m]))
                used.append(slot_ref[3 * side + 2, m] > 0)
        head_bias = []
        for i, (side, r) in enumerate(rows):
            block = sides[3 * side + 2][r]
            block = block if i == 0 else pltpu.roll(block, i * tree, 1)
            here = jnp.logical_and(lane >= i * tree, lane < (i + 1) * tree)
            head_bias.append(jnp.where(here, block, jnp.where(lane < own_keys, NEG_FILL, 0.0)))
        bias = jnp.concatenate(
            [
                jnp.concatenate(head_bias, axis=0) + unseen[:, :lanes],
                jnp.broadcast_to(unseen[:, lanes:], (own_keys, n_keys - lanes)),
            ],
            axis=1,
        )
        results = []
        for h in range(width // HD):
            here = slice(h * HD, (h + 1) * HD)
            held = slice(inside + h * HD, inside + (h + 1) * HD)
            cols = slice(start + h * HD, start + (h + 1) * HD)

            def stored(k):
                own = [sides[3 * side + 1][r, k, :, cols] for side, r in rows]
                return jnp.concatenate(own + [cache[0, k, :, held], cache[1, k, :, held]], axis=0)

            asked = jnp.concatenate([sides[3 * side][r, :, cols] for side, r in rows], axis=0)
            scores = lax.dot_general(
                asked, stored(0), (((1,), (1,)), ((), ())), preferred_element_type=jnp.float32
            )
            scores = scores * (SCALE * LOG2E) + bias
            raw = jnp.exp2(scores - jnp.max(scores, axis=1, keepdims=True))
            total = jnp.sum(raw, axis=1, keepdims=True)
            accum = jnp.dot(raw.astype(jnp.bfloat16), stored(1), preferred_element_type=jnp.float32)
            results.append((here, (accum / total).astype(jnp.bfloat16)))
        for here, attn in results:
            for i, (side, r) in enumerate(rows):
                mine = attn[i * tree : (i + 1) * tree]
                outs[side][r, :, here] = jnp.where(used[i], mine, outs[side][r, :, here])


def attend_pairs(slots, sides, caches, start, inside, width):
    req, tree, _ = sides[0].shape
    vmem = pl.BlockSpec(memory_space=pltpu.VMEM)
    return pl.pallas_call(
        partial(paired_kernel, start=start, inside=inside, n_caches=len(caches)),
        in_specs=[pl.BlockSpec(memory_space=pltpu.SMEM)] + [vmem] * (len(sides) + len(caches)),
        out_specs=[vmem, vmem],
        out_shape=[jax.ShapeDtypeStruct((req, tree, width), jnp.bfloat16)] * 2,
        compiler_params=pltpu.CompilerParams(vmem_limit_bytes=VMEM_BYTES),
        cost_estimate=cost(K_FLOPS + K_FLOPS * width // HD),
    )(slots, *sides, *caches)


def project_kernel(z_ref, w_hbm, *rest, steps, has_acc):
    rest = list(rest)
    acc = rest.pop(0) if has_acc else None
    out_ref, w_ref, sems = rest[-3:]
    z = z_ref[0]
    lower = z < 2
    middle = jnp.logical_and(z > 0, z < 3)
    sources = (z, jnp.bitwise_xor(z, 1), jnp.where(lower, 2, 1), jnp.where(lower, 3, 0))
    copies = []
    at = 0
    for _, _, step in steps:
        for which, start, width in step:
            copies.append(
                pltpu.make_async_copy(
                    w_hbm.at[sources[which], pl.ds(start, width), :],
                    w_ref.at[pl.ds(at, width), :],
                    sems.at[len(copies)],
                )
            )
            copies[-1].start()
            at += width
    pieces = []
    for has_own, has_middle, _ in steps:
        own = rest.pop(0) if has_own else None
        outer = rest.pop(0)
        fresh = own.shape[1] if has_own else 0
        if has_own:
            pieces += [own[...], outer[:, :fresh]]
        if has_middle:
            pieces.append(jnp.where(middle, rest.pop(0)[...], outer[:, fresh:]))
    attn = jnp.concatenate(pieces, axis=1)
    for copy in copies:
        copy.wait()
    tile = 256
    for n in range(out_ref.shape[1] // tile):
        cols = slice(n * tile, (n + 1) * tile)
        total = jnp.dot(attn, w_ref[:, cols], preferred_element_type=jnp.float32)
        if has_acc:
            total += acc[:, cols]
        out_ref[:, cols] = total.astype(out_ref.dtype)


def project(z, weight, steps, acc, last):
    _, _, cols = weight.shape
    given = [] if acc is None else [acc]
    shape = []
    for own, outer, between, parts in steps:
        given += [v for v in (own, outer, between) if v is not None]
        shape.append((own is not None, between is not None, tuple(parts)))
    count = sum(len(step[2]) for step in shape)
    depth = sum(width for step in shape for _, _, width in step[2])
    rows = steps[0][1].shape[0]
    vmem = pl.BlockSpec(memory_space=pltpu.VMEM)
    return pl.pallas_call(
        partial(project_kernel, steps=tuple(shape), has_acc=acc is not None),
        in_specs=[pl.BlockSpec(memory_space=pltpu.SMEM), pl.BlockSpec(memory_space=pltpu.HBM)] + [vmem] * len(given),
        out_specs=vmem,
        out_shape=jax.ShapeDtypeStruct((rows, cols), jnp.bfloat16 if last else jnp.float32),
        scratch_shapes=[
            pltpu.VMEM((depth, cols), jnp.bfloat16),
            pltpu.SemaphoreType.DMA((count,)),
        ],
        input_output_aliases={2: 0} if acc is not None and not last else {},
        compiler_params=pltpu.CompilerParams(vmem_limit_bytes=J_VMEM),
        cost_estimate=cost(J_FLOPS),
    )(z, weight, *given)


def accept_kernel(pick_ref, tree_ref, out_ref):
    for r in range(tree_ref.shape[0]):
        for k in range(2):
            rows = jnp.dot(pick_ref[r], tree_ref[r, k], preferred_element_type=jnp.float32)
            out_ref[r, k] = rows[: out_ref.shape[2]].astype(out_ref.dtype)


def accept(path, tree_cache):
    req, _, tree, cols = tree_cache.shape
    taken = path.shape[1]
    order = jnp.arange(tree, dtype=jnp.int32)
    pick = (path[:, :, None] == order[None, None, :]).astype(jnp.bfloat16)
    pick = jnp.pad(pick, ((0, 0), (0, -taken % 16), (0, 0)))
    vmem = pl.BlockSpec(memory_space=pltpu.VMEM)
    return pl.pallas_call(
        accept_kernel,
        in_specs=[vmem, vmem],
        out_specs=vmem,
        out_shape=jax.ShapeDtypeStruct((req, 2, taken, cols), jnp.bfloat16),
        compiler_params=pltpu.CompilerParams(vmem_limit_bytes=VMEM_BYTES),
        cost_estimate=cost(J_FLOPS),
    )(pick, tree_cache)


def cache_block(prompt, spill, lens, start, width, padded):
    both = jnp.stack([prompt[0, ..., start : start + width], spill[0, ..., start : start + width]])
    both = jnp.pad(both, ((0, 0), (0, 0), (0, padded - both.shape[2]), (0, 0)))
    row = lax.broadcasted_iota(jnp.int32, both.shape, 2)
    return jnp.where(row == padded - 1, lens[:, None, None, None], both)


def across(value, mask):
    return lax.ppermute(value, "rep", [(i, i ^ mask) for i in range(lax.axis_size("rep"))])


def along(value, pairs):
    return lax.ppermute(value, "tp", pairs)


def after(value, *earlier):
    return lax.optimization_barrier((value, *earlier))[0]


def pair_slots(group, blocks):
    match = blocks[:, None] == group[None, :]
    order = jnp.arange(group.shape[0], dtype=jnp.int32)[None, :]
    lowest = jnp.min(jnp.where(match, order, group.shape[0]), axis=1)
    highest = jnp.max(jnp.where(match, order, -1), axis=1)
    used = highest >= 0
    return [jnp.where(used, lowest, 0), jnp.where(used, highest, 0), used.astype(jnp.int32)]


def pair_bias(tree_mask):
    bias = jnp.where(tree_mask == 1, 0.0, NEG_FILL).astype(jnp.float32)
    tree = bias.shape[1]
    return jnp.pad(bias, ((0, 0), (0, 0), (0, -(-4 * tree // HD) * HD - tree)))


def local(
    queries,
    tree_cache,
    tree_mask,
    dest_group,
    accepted_path,
    prompt_cache,
    first_len,
    spill_cache,
    spill_len,
    out_weight,
    *,
    tuned,
):
    req, tree, cols = queries.shape
    prompt = prompt_cache.shape[2]
    padded = (prompt // 16 + 1) * 16
    group = dest_group[:, 0]

    if not tuned:
        accepted_cache = jnp.take_along_axis(tree_cache, accepted_path[:, None, :, None], axis=2)
        lens = jnp.stack([first_len[0], spill_len[0]]).astype(jnp.bfloat16)
        idx = jnp.stack([group, jnp.bitwise_xor(group, 1)])
        bias = jnp.where(tree_mask == 1, 0.0, NEG_FILL).astype(jnp.float32)
        bias = jnp.pad(bias, ((0, 0), (0, 0), (2 * padded, 0)))
        block = cache_block(prompt_cache, spill_cache, lens, 0, cols, padded)
        caches = lax.all_gather(block, "rep", axis=0, tiled=False)
        attn = attend(idx, queries, tree_cache, bias, [caches], 0, cols).reshape(req * tree, cols)
        whole = lax.all_gather(attn, "tp", axis=1, tiled=True)
        summed = jnp.dot(whole, out_weight, preferred_element_type=jnp.float32)
        return summed.astype(jnp.bfloat16).reshape(req, tree, out_weight.shape[1]), accepted_cache

    spill = across(spill_cache, 1)
    lens = jnp.stack([first_len[0], across(spill_len, 1)[0]]).astype(jnp.bfloat16)
    chunks = []
    start = 0
    for heads in HEAD_CHUNKS:
        chunks.append((start, heads * HD))
        start += heads * HD
    n = len(chunks)
    gathered, owns, raws = [], [], []

    def gather(i):
        start, width = chunks[i]
        block = cache_block(prompt_cache, spill, lens, start, width, padded)
        if i > 0:
            block = after(block, *gathered[i - 1][1:])
        gathered.append([block] + [across(block, m) for m in (2, 4, 6)])

    gather(0)
    queries, tree_cache = lax.optimization_barrier((queries, tree_cache, gathered[0][0]))[:2]
    other_queries = across(queries, 1)
    other_tree = across(tree_cache, 1)
    tree_mask, dest_group = lax.optimization_barrier((tree_mask, dest_group, gathered[0][FRONT]))[:2]
    other_mask = across(tree_mask, 1)
    group, other_group = dest_group[:, 0], across(dest_group, 1)[:, 0]
    me = lax.axis_index("rep").astype(jnp.int32)
    blocks = jnp.bitwise_xor(me, jnp.array([0, 2, 4, 6], jnp.int32))
    slots = jnp.stack(pair_slots(group, blocks) + pair_slots(other_group, blocks))
    sides = [queries, tree_cache, pair_bias(tree_mask), other_queries, other_tree, pair_bias(other_mask)]
    mine = jnp.bitwise_and(jnp.bitwise_xor(group, me), 1) == 0

    z = lax.axis_index("tp").astype(jnp.int32).reshape(1)
    weight = out_weight.reshape(lax.axis_size("tp"), cols, out_weight.shape[1])
    acc = None
    steps, outer, between = [], [], []
    for i in range(n + 2):
        fresh = []
        if i < n:
            start, width = chunks[i]
            ready = slots
            if i > 0:
                gates = [owns[i - 1]] + between[max(i - 2, 0) : i - 1]
                ready = after(slots, *gates)
            own, theirs = attend_pairs(ready, sides, gathered[i], start, 0, width)
            raws.append(theirs)
            if i + 1 < n:
                gather(i + 1)
            if i > 0:
                theirs = after(theirs, between[i - 1])
            if 0 < i < n - 1:
                theirs = after(theirs, outer[i - 1])
            attn = jnp.where(mine[:, None, None], own, across(theirs, 1)).reshape(req * tree, width)
            owns.append(attn)
            fresh = [attn]
        payload = fresh + ([between[i - 1]] if i > 0 else [])
        payload = jnp.concatenate(payload, axis=1)
        outer.append(along(payload, [(0, 1), (1, 0), (2, 3), (3, 2)] if i < n else [(1, 0), (2, 3)]))
        if i <= n:
            relayed = [outer[i - 1][:, : chunks[i - 1][1]]] if i > 0 else []
            between.append(along(jnp.concatenate(fresh + relayed, axis=1), [(1, 2), (2, 1)]))
        parts = [(0, *chunks[i]), (1, *chunks[i])] if i < n else []
        parts += [(2, *chunks[i - 1])] if 0 < i <= n else []
        parts += [(3, *chunks[i - 2])] if i > 1 else []
        steps.append(
            (owns[i] if i < n else None, outer[i], between[i - 1] if i > 0 else None, parts)
        )
        if i in SPLITS:
            acc = project(after(z, raws[-1]), weight, steps, acc, i == n + 1)
            steps = []
    path = after(accepted_path, outer[n - 1])
    accepted_cache = accept(path, tree_cache)
    return acc.reshape(req, tree, out_weight.shape[1]), accepted_cache


def solution(mesh):
    heads_here = 32 // mesh.shape["tp"]
    tuned = mesh.shape["rep"] == 8 and mesh.shape["tp"] == 4 and heads_here == sum(HEAD_CHUNKS)
    return jax.shard_map(
        partial(local, tuned=tuned),
        mesh=mesh,
        in_specs=(
            P("rep", None, "tp"),
            P("rep", None, None, "tp"),
            P("rep", None, None),
            P("rep", None),
            P("rep", None),
            P("rep", None, None, "tp"),
            P("rep"),
            P("rep", None, None, "tp"),
            P("rep"),
            P(None, "tp"),
        ),
        out_specs=(P("rep", None, "tp"), P("rep", None, None, "tp")),
        check_vma=False,
    )
```
